128 devices in a mesh: dp: 8 (over z, core), ctx: 4 (over x), tensor: 4 (over y).
Axes of the slice: x: 4, y: 4, z: 4, core: 2. Of those that a mesh axis runs over, the one named last changes fastest.
Arguments:
- tokens: bfloat16 [8192, 2048], P(('dp', 'ctx')), may hold values from -6 to 6
- cotangent: bfloat16 [8192, 2048], P(('dp', 'ctx')), may hold values from -6 to 6
- segments: int32 [8, 1024], P('dp'), may hold values from 0 to 2, as said below
- owners: int32 [7, 32], replicated, may hold values from 0 to 31, each once within a row
- gains: float32 [2, 2048], replicated, may hold values from 0.5 to 1.5
- gain_moments: float32 [2, 2048], P(None, ('dp', 'ctx')), may hold values from -256 to 256
- query_master: float32 [2048, 2048], P(('dp', 'ctx'), 'tensor'), may hold values from -0.125 to 0.125
- key_master_blocks: float32 [2048, 512], P(('dp', 'ctx'), 'tensor'), may hold values from -0.125 to 0.125
- value_master_blocks: float32 [2048, 512], P(('dp', 'ctx'), 'tensor'), may hold values from -0.125 to 0.125
- output_master: float32 [2048, 2048], P(('dp', 'ctx'), 'tensor'), may hold values from -0.5 to 0.5
- gate_master: float32 [2048, 8192], P(('dp', 'ctx'), 'tensor'), may hold values from -0.125 to 0.125
- up_master: float32 [2048, 8192], P(('dp', 'ctx'), 'tensor'), may hold values from -0.125 to 0.125
- down_master: float32 [2048, 8192], P(('dp', 'ctx'), 'tensor'), may hold values from -0.09375 to 0.09375
- query_moment: float32 [2048, 2048], P(('dp', 'ctx'), 'tensor'), may hold values from -256 to 256
- key_momentum: float32 [2048, 512], P(('dp', 'ctx'), 'tensor'), may hold values from -256 to 256
- value_momentum: float32 [2048, 512], P(('dp', 'ctx'), 'tensor'), may hold values from -256 to 256
- output_moment: float32 [2048, 2048], P(('dp', 'ctx'), 'tensor'), may hold values from -256 to 256
- gate_moment: float32 [2048, 8192], P(('dp', 'ctx'), 'tensor'), may hold values from -256 to 256
- up_moment: float32 [2048, 8192], P(('dp', 'ctx'), 'tensor'), may hold values from -256 to 256
- down_moment: float32 [2048, 8192], P(('dp', 'ctx'), 'tensor'), may hold values from -256 to 256
Outputs:
- output: bfloat16 [8192, 2048], P(('dp', 'ctx'))
- grad_input: float32 [8192, 2048], P(('dp', 'ctx'))
- new_query: float32 [2048, 2048], P(('dp', 'ctx'), 'tensor')
- new_key: float32 [2048, 512], P(('dp', 'ctx'), 'tensor')
- new_value: float32 [2048, 512], P(('dp', 'ctx'), 'tensor')
- new_output: float32 [2048, 2048], P(('dp', 'ctx'), 'tensor')
- new_gate: float32 [2048, 8192], P(('dp', 'ctx'), 'tensor')
- new_up: float32 [2048, 8192], P(('dp', 'ctx'), 'tensor')
- new_down: float32 [2048, 8192], P(('dp', 'ctx'), 'tensor')
- query_moment_out: float32 [2048, 2048], P(('dp', 'ctx'), 'tensor')
- key_moment_out: float32 [2048, 512], P(('dp', 'ctx'), 'tensor')
- value_moment_out: float32 [2048, 512], P(('dp', 'ctx'), 'tensor')
- output_moment_out: float32 [2048, 2048], P(('dp', 'ctx'), 'tensor')
- gate_moment_out: float32 [2048, 8192], P(('dp', 'ctx'), 'tensor')
- up_moment_out: float32 [2048, 8192], P(('dp', 'ctx'), 'tensor')
- down_moment_out: float32 [2048, 8192], P(('dp', 'ctx'), 'tensor')
- new_gains: float32 [2, 2048], P(None, ('dp', 'ctx'))
- gain_moments_out: float32 [2, 2048], P(None, ('dp', 'ctx'))
The draws below stay inside these ranges and needn't reach their ends.
Inputs may be any that keep to these rules, and one draw needn't show every extreme that they name: `segments`: each packed sequence holds exactly three documents, numbered 0, 1, 2 in order; document 1 reaches from the first 256 tokens to the last 256. `owners`: each row names every owner 0 to 31 exactly once.
All inputs are finite; a program needn't handle non-finite values.
Results may differ from the reference program's by a relative error of at most 0.02.
Values may be sent and summed in bfloat16 or wider, within the bound.
A program may use at most 192 MiB of HBM per device.

```python
import math
import jax
import jax.numpy as jnp
from jax import lax

MODEL_WIDTH = 2048
QUERY_HEAD_COUNT = 32
KEY_VALUE_HEADS = 8
HEAD_SIZE = 64
FF = 8192
TOK_DEV = 256
SEQ = 1024
TOKEN_TOTAL = 8192
NB = 32
BR = 64
N_DP = 8
N_CTX = 4
N_TENSOR = 4


def draw_segments(key, part):
    key = jax.random.fold_in(key, 7)
    start_key, end_key = jax.random.split(key, 2)
    places = jnp.arange(SEQ, dtype=jnp.int32)[None, :]
    long_start = jax.random.randint(start_key, (N_DP, 1), 1, TOK_DEV)
    long_end = jax.random.randint(end_key, (N_DP, 1), (N_CTX - 1) * TOK_DEV + 1, SEQ)
    starts = (places == long_start) | (places == long_end)
    return jnp.cumsum(starts.astype(jnp.int32), axis=1).astype(jnp.int32)


def block_levels(rng, dims, shards, low, high):
    def one(axis_at, blocks):
        draws = jax.random.uniform(jax.random.fold_in(jax.random.fold_in(rng, 6), axis_at), (blocks,), jnp.float32, low / len(shards), high / len(shards))
        return jnp.repeat(jnp.exp(draws), dims[axis_at] // blocks).reshape((-1,) + (1,) * (len(dims) - axis_at - 1))

    level = one(*shards[0])
    for cut in shards[1:]:
        level = level * one(*cut)
    return level


def bell_draw(stream_key, shape, spread, reach, cuts=(), held_as=jnp.bfloat16):
    factor_of = block_levels(stream_key, shape, cuts, -0.22, 0.18) if cuts else 1.0
    drawn = jax.random.normal(stream_key, shape, jnp.float32) * spread * factor_of
    return jnp.minimum(jnp.maximum(drawn, -reach), reach).astype(held_as)


def setup_inputs(seed: int = 0) -> dict:
    keys = jax.random.split(jax.random.key(seed), 21)
    tokens = bell_draw(keys[0], (TOKEN_TOTAL, MODEL_WIDTH), 1.0, 6.0, ((0, 32),))
    cotangent = bell_draw(keys[1], (TOKEN_TOTAL, MODEL_WIDTH), 1.0, 6.0, ((0, 32),))
    segments = draw_segments(jax.random.fold_in(keys[20], 71), 0)
    owners = jax.vmap(lambda own: jax.random.permutation(own, NB))(jax.random.split(keys[3], 7)).reshape((7, NB)).astype(jnp.int32)
    gains = jnp.clip(1.0 + 0.1 * jax.random.normal(keys[4], (2, MODEL_WIDTH), jnp.float32), 0.5, 1.5)
    gain_moments = bell_draw(keys[5], (2, MODEL_WIDTH), (0.5 * TOKEN_TOTAL ** 0.5), 256.0, ((1, 32),), jnp.float32)
    query_master = bell_draw(keys[6], (MODEL_WIDTH, QUERY_HEAD_COUNT * HEAD_SIZE), MODEL_WIDTH ** -0.5, 0.125, ((0, 32), (1, 4)), jnp.float32)
    key_master_blocks = bell_draw(keys[7], (MODEL_WIDTH, KEY_VALUE_HEADS * HEAD_SIZE), MODEL_WIDTH ** -0.5, 0.125, ((0, 32), (1, 4)), jnp.float32)
    value_master_blocks = bell_draw(keys[8], (MODEL_WIDTH, KEY_VALUE_HEADS * HEAD_SIZE), MODEL_WIDTH ** -0.5, 0.125, ((0, 32), (1, 4)), jnp.float32)
    output_master = bell_draw(keys[9], (MODEL_WIDTH, QUERY_HEAD_COUNT * HEAD_SIZE), (QUERY_HEAD_COUNT * HEAD_SIZE // 16) ** -0.5, 0.5, ((0, 32), (1, 4)), jnp.float32)
    gate_master = bell_draw(keys[10], (MODEL_WIDTH, FF), MODEL_WIDTH ** -0.5, 0.125, ((0, 32), (1, 4)), jnp.float32)
    up_master = bell_draw(keys[11], (MODEL_WIDTH, FF), MODEL_WIDTH ** -0.5, 0.125, ((0, 32), (1, 4)), jnp.float32)
    down_master = bell_draw(keys[12], (MODEL_WIDTH, FF), (FF // 2) ** -0.5, 0.09375, ((0, 32), (1, 4)), jnp.float32)
    query_moment = bell_draw(keys[13], (MODEL_WIDTH, QUERY_HEAD_COUNT * HEAD_SIZE), (0.5 * TOKEN_TOTAL ** 0.5), 256.0, ((0, 32), (1, 4)), jnp.float32)
    key_momentum = bell_draw(keys[14], (MODEL_WIDTH, KEY_VALUE_HEADS * HEAD_SIZE), (0.5 * TOKEN_TOTAL ** 0.5), 256.0, ((0, 32), (1, 4)), jnp.float32)
    value_momentum = bell_draw(keys[15], (MODEL_WIDTH, KEY_VALUE_HEADS * HEAD_SIZE), (0.5 * TOKEN_TOTAL ** 0.5), 256.0, ((0, 32), (1, 4)), jnp.float32)
    output_moment = bell_draw(keys[16], (MODEL_WIDTH, QUERY_HEAD_COUNT * HEAD_SIZE), (0.5 * TOKEN_TOTAL ** 0.5), 256.0, ((0, 32), (1, 4)), jnp.float32)
    gate_moment = bell_draw(keys[17], (MODEL_WIDTH, FF), (0.5 * TOKEN_TOTAL ** 0.5), 256.0, ((0, 32), (1, 4)), jnp.float32)
    up_moment = bell_draw(keys[18], (MODEL_WIDTH, FF), (0.5 * TOKEN_TOTAL ** 0.5), 256.0, ((0, 32), (1, 4)), jnp.float32)
    down_moment = bell_draw(keys[19], (MODEL_WIDTH, FF), (0.5 * TOKEN_TOTAL ** 0.5), 256.0, ((0, 32), (1, 4)), jnp.float32)
    return dict(tokens=tokens, cotangent=cotangent, segments=segments, owners=owners, gains=gains, gain_moments=gain_moments, query_master=query_master, key_master_blocks=key_master_blocks, value_master_blocks=value_master_blocks, output_master=output_master, gate_master=gate_master, up_master=up_master, down_master=down_master, query_moment=query_moment, key_momentum=key_momentum, value_momentum=value_momentum, output_moment=output_moment, gate_moment=gate_moment, up_moment=up_moment, down_moment=down_moment)


@jax.custom_vjp
def low(v):
    return lax.optimization_barrier(v.astype(jnp.bfloat16)).astype(jnp.float32)

@jax.custom_vjp
def low_back(v):
    return v

def low_keep(v):
    return (low(v), None)

def low_pass(kept, grad):
    return (grad,)

def back_keep(v):
    return (v, None)

def back_low(kept, grad):
    return (low(grad),)
low.defvjp(low_keep, low_pass)
low_back.defvjp(back_keep, back_low)
norm_epsilon = 1e-05
rope_base = 500000.0
momentum_decay = 0.95
learning_rate = 0.1
weight_decay = 0.01
gain_rate = 0.001
newton_coeffs = (3.4445, -4.775, 2.0315)
masked_score = -1e+30
highest = lax.Precision.HIGHEST

def rope_frequencies(head_dim):
    even = jnp.arange(0, head_dim, 2, dtype=jnp.float32)
    base_rates = 1.0 / rope_base ** (even / head_dim)
    wavelength = 2.0 * math.pi / base_rates
    smooth = (8192.0 / wavelength - 1.0) / 3.0
    blended = (1.0 - smooth) * base_rates / 32.0 + smooth * base_rates
    return jnp.where(wavelength < 2048.0, base_rates, jnp.where(wavelength > 8192.0, base_rates / 32.0, blended))

def rope_tables(places, head_dim):
    angles = places.astype(jnp.float32)[:, None] * rope_frequencies(head_dim)[None, :]
    angles = jnp.concatenate([angles, angles], axis=-1)
    return (jnp.cos(angles), jnp.sin(angles))

def apply_rotary(value_rows, cosine_table, sine_table):
    half = value_rows.shape[-1] // 2
    turned = jnp.concatenate([-value_rows[..., half:], value_rows[..., :half]], axis=-1)
    return value_rows * cosine_table[:, None, :] + turned * sine_table[:, None, :]

def document_places(segment_ids):
    count = segment_ids.shape[0]
    places = jnp.arange(count, dtype=jnp.int32)
    change = jnp.concatenate([jnp.ones((1,), dtype=bool), segment_ids[1:] != segment_ids[:-1]])
    starts = lax.cummax(jnp.where(change, places, 0), axis=0)
    return places - starts

def root_scale(value_rows):
    return lax.rsqrt(lax.optimization_barrier(jnp.mean(value_rows * value_rows, axis=-1, keepdims=True)) + norm_epsilon)

def natural_order(stored, order):
    count = order.shape[0]
    whole = stored.reshape(count, -1, stored.shape[1])
    return jnp.take(whole, order, axis=0).reshape(stored.shape)

def owner_order(value_rows, order):
    count = order.shape[0]
    slots = lax.optimization_barrier(jnp.sum(jnp.where(order[:, None] == jnp.arange(count, dtype=jnp.int32)[None, :], jnp.arange(count, dtype=jnp.int32)[:, None], 0), axis=0)).astype(jnp.int32)
    whole = value_rows.reshape(count, -1, value_rows.shape[1])
    return jnp.take(whole, slots, axis=0).reshape(value_rows.shape)

def orthogonalize(matrix):
    first, second, third = newton_coeffs
    tall = matrix.shape[-2] > matrix.shape[-1]
    current = jnp.swapaxes(matrix, -1, -2) if tall else matrix
    current = current / (jnp.sqrt(lax.optimization_barrier(jnp.sum(current * current, axis=(-2, -1), keepdims=True))) + 1e-07)
    for sweep in range(5):
        gram = jnp.einsum('...ik,...jk->...ij', current, current, precision=highest)
        mixed = second * gram + third * jnp.einsum('...ij,...jk->...ik', gram, gram, precision=highest)
        current = first * current + jnp.einsum('...ij,...jk->...ik', mixed, current, precision=highest)
    return jnp.swapaxes(current, -1, -2) if tall else current

def muon_block(master, moment, grad):
    renewed = momentum_decay * moment + grad
    direction = orthogonalize(grad + momentum_decay * renewed)
    factor = 0.2 * math.sqrt(max(master.shape[-2], master.shape[-1]))
    return (master * (1.0 - learning_rate * weight_decay) - learning_rate * factor * direction, renewed)

def attend(query_lowered, key_lowered, value_lowered, segment_ids):
    sequence_length = segment_ids.shape[0]
    query_groups = query_lowered.reshape(sequence_length, KEY_VALUE_HEADS, QUERY_HEAD_COUNT // KEY_VALUE_HEADS, HEAD_SIZE)
    scores = low_back(jnp.einsum('qhgd,khd->hgqk', query_groups, key_lowered, precision=highest))
    places = jnp.arange(sequence_length, dtype=jnp.int32)
    allowed = (segment_ids[:, None] == segment_ids[None, :]) & (places[None, :] <= places[:, None])
    masked = jnp.where(allowed, scores, masked_score)
    log_norm = jax.nn.logsumexp(masked, axis=-1)
    probs = low(jnp.where(allowed, jnp.exp(masked - log_norm[..., None]), 0.0))
    attended = jnp.einsum('hgqk,khd->qhgd', probs, value_lowered, precision=highest)
    return attended.reshape(sequence_length, QUERY_HEAD_COUNT * HEAD_SIZE)

def forward_sequence(residual_in, gain_values, query_weight, key_weight, value_weight, output_weight, gate_weight, up_weight, down_weight, segment_ids):
    sequence_length = residual_in.shape[0]
    cosine_table, sine_table = rope_tables(document_places(segment_ids), HEAD_SIZE)
    normed_one = low(residual_in * root_scale(residual_in) * gain_values[0])
    queries = low_back(jnp.dot(normed_one, query_weight, precision=highest))
    key_rows = low_back(jnp.dot(normed_one, key_weight, precision=highest))
    value_rows = low_back(jnp.dot(normed_one, value_weight, precision=highest))
    query_lowered = low(apply_rotary(queries.reshape(sequence_length, QUERY_HEAD_COUNT, HEAD_SIZE), cosine_table, sine_table) * HEAD_SIZE ** (-0.5))
    key_lowered = low(apply_rotary(key_rows.reshape(sequence_length, KEY_VALUE_HEADS, HEAD_SIZE), cosine_table, sine_table))
    value_lowered = low(value_rows.reshape(sequence_length, KEY_VALUE_HEADS, HEAD_SIZE))
    attended = low(low_back(jax.checkpoint(attend)(query_lowered, key_lowered, value_lowered, segment_ids)))
    attention_out = low_back(jnp.dot(attended, output_weight.T, precision=highest))
    residual_mid = residual_in + attention_out
    normed_two = low(residual_mid * root_scale(residual_mid) * gain_values[1])
    gate_pre = low_back(jnp.dot(normed_two, gate_weight, precision=highest))
    up_pre = low_back(jnp.dot(normed_two, up_weight, precision=highest))
    hidden = low(jax.nn.silu(gate_pre) * up_pre)
    return residual_mid + low_back(jnp.dot(hidden, down_weight.T, precision=highest))

def split_blocks(value_rows):
    columns = value_rows.shape[1]
    return value_rows.reshape(NB, BR, N_TENSOR, columns // N_TENSOR).transpose(0, 2, 1, 3)

def join_blocks(value_rows):
    return value_rows.transpose(0, 2, 1, 3).reshape(MODEL_WIDTH, -1)

def reference(tokens, cotangent, segments, owners, gains, gain_moments, query_master, key_master_blocks, value_master_blocks, output_master, gate_master, up_master, down_master, query_moment, key_momentum, value_momentum, output_moment, gate_moment, up_moment, down_moment):
    masters = (query_master, key_master_blocks, value_master_blocks, output_master, gate_master, up_master, down_master)
    moments = (query_moment, key_momentum, value_momentum, output_moment, gate_moment, up_moment, down_moment)
    natural = tuple((natural_order(masters[place], owners[place]) for place in range(7)))
    rounded = tuple((lax.optimization_barrier(weight.astype(jnp.bfloat16)).astype(jnp.float32) for weight in natural))
    inputs_all = tokens.astype(jnp.float32).reshape(N_DP, SEQ, MODEL_WIDTH)
    back_all = cotangent.astype(jnp.float32).reshape(N_DP, SEQ, MODEL_WIDTH)

    def one_sequence(totals, pieces):
        residual_in, back, segment_ids = pieces

        def forward(value_rows, gain_values, query_weight, key_weight, value_weight, output_weight, gate_weight, up_weight, down_weight):
            return forward_sequence(value_rows, gain_values, query_weight, key_weight, value_weight, output_weight, gate_weight, up_weight, down_weight, segment_ids)
        result, pullback = jax.vjp(forward, residual_in, gains, rounded[0], rounded[1], rounded[2], rounded[3], rounded[4], rounded[5], rounded[6])
        grads = pullback(back)
        totals = tuple((total + grad for total, grad in zip(totals, grads[1:])))
        return (totals, (result.astype(jnp.bfloat16), grads[0]))
    start = (jnp.zeros(gains.shape, jnp.float32),) + tuple((jnp.zeros(weight.shape, jnp.float32) for weight in natural))
    totals, (outputs, input_grads) = lax.scan(one_sequence, start, (inputs_all, back_all, segments))
    new_masters = []
    new_moments = []
    for place in range(7):
        moment_natural = natural_order(moments[place], owners[place])
        updated, renewed = muon_block(split_blocks(natural[place]), split_blocks(moment_natural), split_blocks(totals[place + 1]))
        new_masters.append(owner_order(join_blocks(updated), owners[place]))
        new_moments.append(owner_order(join_blocks(renewed), owners[place]))
    gain_grad = totals[0]
    new_gain_moments = momentum_decay * gain_moments + gain_grad
    new_gains = gains - gain_rate * (gain_grad + momentum_decay * new_gain_moments)
    return (outputs.reshape(TOKEN_TOTAL, MODEL_WIDTH), input_grads.reshape(TOKEN_TOTAL, MODEL_WIDTH), new_masters[0], new_masters[1], new_masters[2], new_masters[3], new_masters[4], new_masters[5], new_masters[6], new_moments[0], new_moments[1], new_moments[2], new_moments[3], new_moments[4], new_moments[5], new_moments[6], new_gains, new_gain_moments)
```

```python
import math

import jax
import jax.numpy as jnp
import numpy as np
from jax import lax
from jax.experimental import pallas as pl
from jax.experimental.pallas import tpu as pltpu
from jax.sharding import PartitionSpec as P

HEAD_SIZE = 64
WIDTH = 2048
SCALE = HEAD_SIZE ** (-0.5)

norm_epsilon = 1e-05
rope_base = 500000.0
momentum_decay = 0.95
learning_rate = 0.1
weight_decay = 0.01
gain_rate = 0.001
newton_coeffs = (3.4445, -4.775, 2.0315)
masked_score = -1e30

MESH = pl.DeviceIdType.MESH
VMEM_BYTES = 62 * 1024 * 1024
BF16, F32 = jnp.bfloat16, jnp.float32
ANYWHERE = pl.BlockSpec(memory_space=pl.ANY)
IN_VMEM = pl.BlockSpec(memory_space=pltpu.VMEM)
IN_SMEM = pl.BlockSpec(memory_space=pltpu.SMEM)


def rope_frequencies(head_dim):
    even = np.arange(0, head_dim, 2, dtype=np.float32)
    base_rates = np.float32(1.0) / np.float32(rope_base) ** (even / np.float32(head_dim))
    wavelength = np.float32(2.0 * math.pi) / base_rates
    smooth = (np.float32(8192.0) / wavelength - np.float32(1.0)) / np.float32(3.0)
    low_rates = base_rates / np.float32(32.0)
    blended = (np.float32(1.0) - smooth) * low_rates + smooth * base_rates
    return np.where(
        wavelength < 2048.0, base_rates, np.where(wavelength > 8192.0, low_rates, blended)
    ).astype(np.float32)


def wide(value):
    return value.astype(F32)


def narrow(value):
    return value.astype(BF16)


def times(left, right, contract=((1,), (0,))):
    return lax.dot_general(left, right, (contract, ((), ())), preferred_element_type=F32)


LAST = ((1,), (1,))


def wrap(value):
    return lax.rem(value + 4, 4)


class Place:
    def __init__(self):
        self.dp = lax.axis_index("dp")
        self.x = lax.axis_index("ctx")
        self.y = lax.axis_index("tensor")
        self.z = lax.div(self.dp, 2)
        self.core = lax.rem(self.dp, 2)
        self.known = {}

    def at(self, axis):
        return {"x": self.x, "y": self.y, "z": self.z}[axis]

    def toward(self, axis, step):
        if (axis, step) not in self.known:
            self.known[axis, step] = self.reach(axis, step)
        return self.known[axis, step]

    def reach(self, axis, step):
        if axis == "x":
            return (self.dp, wrap(self.x + step), self.y)
        if axis == "y":
            return (self.dp, self.x, wrap(self.y + step))
        if axis == "z":
            return (wrap(self.z + step) * 2 + self.core, self.x, self.y)
        return (self.z * 2 + 1 - self.core, self.x, self.y)


class Wire:
    def __init__(self, place, send_sem, recv_sem):
        self.place, self.send_sem, self.recv_sem = place, send_sem, recv_sem
        self.count, self.open = 0, []

    def send(self, source, target, axis, step):
        copy = pltpu.make_async_remote_copy(
            src_ref=source,
            dst_ref=target,
            send_sem=self.send_sem.at[self.count],
            recv_sem=self.recv_sem.at[self.count],
            device_id=self.place.toward(axis, step),
            device_id_type=MESH,
        )
        copy.start()
        self.count += 1
        self.open.append(copy)
        return copy

    def sent(self, copies):
        for copy in copies:
            copy.wait_send()
            self.open = [other for other in self.open if other is not copy]

    def finish(self):
        for copy in self.open:
            copy.wait_send()


class Local:
    def __init__(self, sem):
        self.sem, self.count, self.open = sem, 0, []

    def copy(self, source, target):
        copy = pltpu.make_async_copy(source, target, self.sem.at[self.count])
        copy.start()
        self.count += 1
        self.open.append(copy)
        return copy

    def done(self, *copies):
        for copy in copies:
            copy.wait()
            self.open = [other for other in self.open if other is not copy]

    def finish(self):
        self.done(*self.open)


def greet(place, partners):
    barrier = pltpu.get_barrier_semaphore()
    for axis, step in partners:
        pl.semaphore_signal(
            barrier, inc=1, device_id=place.toward(axis, step), device_id_type=MESH
        )
    pl.semaphore_wait(barrier, len(partners))


PARTNERS = (
    ("x", 1),
    ("x", -1),
    ("z", 1),
    ("z", -1),
    ("core", 1),
    ("y", 1),
    ("y", -1),
    ("x", 2),
    ("y", 2),
)


class Course:
    def __init__(self, table):
        self.table, self.count, self.flows = table, 0, []

    def add(self, flow, turn=0):
        self.flows.append(flow)
        return len(self.flows) - 1

    def step(self, number):
        if next(self.flows[number], None) is None:
            self.flows[number] = iter(())

    def point(self):
        if self.count < len(self.table):
            for number in self.table[self.count]:
                self.step(number)
        self.count += 1

    def until(self, numbers):
        self.point()
        for number in numbers:
            for _ in self.flows[number]:
                pass
            self.flows[number] = iter(())


FULL, LOW, HIGH = pl.ds(0, 4), pl.ds(0, 2), pl.ds(2, 2)


def gather_chunk(wire, whole, low, width, first, gaps=(1, 1, 1, 1, 1)):
    place = wire.place
    second = "z" if first == "x" else "x"
    own, other, core = place.at(first), place.at(second), place.core
    cut = pl.ds(low, width)
    every, low_rows, high_rows = pl.ds(0, 64), pl.ds(0, 32), pl.ds(32, 32)

    def block(spot, rows):
        if first == "x":
            return whole.at[other, core, spot, rows, cut]
        return whole.at[spot, core, other, rows, cut]

    def line(spot, part):
        if first == "x":
            return whole.at[spot, core, part, :, cut]
        return whole.at[part, core, spot, :, cut]

    def go(ref, axis, step):
        return wire.send(ref, ref, axis, step)

    right = go(block(own, every), first, 1)
    left = go(block(own, every), first, -1)
    yield gaps[0]
    right.wait_recv()
    left.wait_recv()
    right = go(block(wrap(own - 1), low_rows), first, 1)
    left = go(block(wrap(own + 1), high_rows), first, -1)
    yield gaps[1]
    right.wait_recv()
    left.wait_recv()
    right = go(line(other, FULL), second, 1)
    left = go(line(other, FULL), second, -1)
    across = [go(line(other, FULL), "core", 1)]
    yield gaps[2]
    right.wait_recv()
    left.wait_recv()
    before, after = wrap(other - 1), wrap(other + 1)
    right = go(line(before, LOW), second, 1)
    left = go(line(after, HIGH), second, -1)
    across.append(go(line(before, FULL), "core", 1))
    across.append(go(line(after, FULL), "core", 1))
    yield gaps[3]
    right.wait_recv()
    left.wait_recv()
    across.append(go(line(wrap(other + 2), FULL), "core", 1))
    yield gaps[4]
    for copy in across:
        copy.wait_recv()


def cuts(width, parts):
    return [pl.ds(part * (width // parts), width // parts) for part in range(parts)]


def ring_sum(wire, axis, mine, near, far, parts=2):
    own = wire.place.at(axis)
    before, after, facing = wrap(own - 1), wrap(own + 1), wrap(own + 2)
    half = mine.shape[1] // 2
    low_rows, high_rows = pl.ds(0, half), pl.ds(half, half)
    flights = []
    for cut in cuts(mine.shape[2], parts):
        right = wire.send(mine.at[facing, low_rows, cut], near.at[0, :, cut], axis, 1)
        left = wire.send(mine.at[facing, high_rows, cut], near.at[1, :, cut], axis, -1)
        flights.append((cut, right, left))
        yield 1
    second = []
    for cut, right, left in flights:
        right.wait_recv()
        left.wait_recv()
        mine[after, low_rows, cut] = mine[after, low_rows, cut] + near[0, :, cut]
        mine[before, high_rows, cut] = mine[before, high_rows, cut] + near[1, :, cut]
        right = wire.send(mine.at[after, :, cut], far.at[0, :, cut], axis, 1)
        left = wire.send(mine.at[before, :, cut], far.at[1, :, cut], axis, -1)
        second.append((right, left))
    yield 1
    for right, left in second:
        right.wait_recv()
        left.wait_recv()


def ring_total(wire, axis, mine, far):
    return wide(mine[wire.place.at(axis)]) + wide(far[0]) + wide(far[1])


def ring_spread(wire, axis, whole, parts=2):
    own = wire.place.at(axis)
    before, after = wrap(own - 1), wrap(own + 1)
    half = whole.shape[1] // 2
    low_rows, high_rows = pl.ds(0, half), pl.ds(half, half)

    def go(ref, step):
        return wire.send(ref, ref, axis, step)

    flights = []
    for cut in cuts(whole.shape[2], parts):
        flights.append((cut, go(whole.at[own, :, cut], 1), go(whole.at[own, :, cut], -1)))
    yield 1
    second = []
    for cut, right, left in flights:
        right.wait_recv()
        left.wait_recv()
        second.append(go(whole.at[before, low_rows, cut], 1))
        second.append(go(whole.at[after, high_rows, cut], -1))
    yield 1
    for copy in second:
        copy.wait_recv()


def owner_spot(owners, matrix, block):
    owner = owners[matrix, block]
    return lax.div(owner, 8), lax.rem(lax.div(owner, 4), 2), lax.rem(owner, 4)


def natural_rows(whole, owners, matrix, block, count, cut):
    return jnp.concatenate(
        [whole[(*owner_spot(owners, matrix, block + index), slice(None), cut)] for index in range(count)],
        axis=0,
    )


def columns(index, size):
    return pl.ds(pl.multiple_of(index * size, size), size)


def loop(count, body):
    def step(index, carry):
        body(index)
        return carry

    lax.fori_loop(0, count, step, 0)


def identity(size):
    row = lax.broadcasted_iota(jnp.int32, (size, size), 0)
    return narrow(jnp.where(row == lax.broadcasted_iota(jnp.int32, (size, size), 1), 1.0, 0.0))


def transpose_into(target, source):
    def slab(index):
        part = source[:, :, :, columns(index, 256)].reshape(256, 256)
        target[pl.ds(index * 4, 4)] = narrow(times(identity(256), part, LAST)).reshape(4, 64, 256)

    loop(8, slab)


def root_scale(value):
    return lax.rsqrt(jnp.mean(value * value, axis=-1, keepdims=True) + norm_epsilon)


def swap_halves(value):
    lane = lax.broadcasted_iota(jnp.int32, value.shape, 1)
    return jnp.where(
        lax.rem(lane, 64) < 32, pltpu.roll(value, 96, 1), pltpu.roll(value, 32, 1)
    )


def signs(shape):
    lane = lax.broadcasted_iota(jnp.int32, shape, 1)
    return jnp.where(lax.rem(lane, 64) < 32, -1.0, 1.0)


def rotate(value, cosine, sine):
    return value * cosine + swap_halves(value) * (sine * signs(value.shape))


def rotate_back(value, cosine, sine):
    return value * cosine - swap_halves(value * sine) * signs(value.shape)


EAGER = 3
FORWARD_COURSE = (
    (0, 1, 2, 3),
    (6, 7, 8),
    (0, 1, 2, 3, 5, 4),
    (6, 7),
    (1, 8, 0, 3, 2, 5, 4, 1, 0, 6, 12, 13, 14, 2, 5, 3, 4, 0, 1, 0, 1),
    (),
    (15, 16, 17),
    (9, 10, 11, 5, 13, 3, 2, 3, 2),
    (12,),
    (14,),
    (4,),
    (15,),
    (17, 9, 11, 16, 6),
    (5, 4, 7, 8, 10),
    (5, 4),
    (),
    (),
    (6, 9),
    (6, 12),
    (7,),
    (8,),
    (),
    (9,),
    (10, 7, 11),
    (),
    (),
    (7, 8, 12, 9),
    (8, 13, 9),
    (),
    (10,),
    (12, 11, 14, 12),
    (),
    (10, 13),
    (10, 15, 16),
    (11,),
    (11, 13, 14),
    (),
    (13, 17),
    (16,),
    (15, 14),
    (14,),
    (),
    (16, 17),
    (16,),
    (15,),
    (15, 17),
    (),
    (17,),
    (),
    (),
    (),
    (),
)


def forward_body(
    in_tokens,
    in_cotangent,
    segments,
    owners,
    owner_rows,
    gains,
    rates,
    m_query,
    m_key,
    m_value,
    m_output,
    m_gate,
    m_up,
    m_down,
    out_w_q,
    out_w_kv,
    out_w_out,
    out_mid,
    out_n1_t,
    out_n2,
    out_back_t,
    out_hidden,
    out_d_gate,
    out_d_up,
    out_dn,
    out_f,
    out_probs,
    out_q,
    out_kv,
    out_attended,
    out_tables,
    out_slots,
    tokens,
    cotangent,
    w_q,
    w_kv,
    w_out,
    w_gate_0,
    w_gate_1,
    w_gate_2,
    w_gate_3,
    w_up_0,
    w_up_1,
    w_up_2,
    w_up_3,
    w_down_0,
    w_down_1,
    w_down_2,
    w_down_3,
    mid_out,
    flip,
    hidden,
    d_gate,
    d_up,
    probs,
    q_out,
    kv,
    attended,
    tables,
    normed,
    normed_two,
    f_sum,
    dn_sum,
    near,
    far,
    bias,
    q_t8,
    v_t,
    o_t,
    local_sem,
    send_sem,
    recv_sem,
):
    place = Place()
    w_gate = (w_gate_0, w_gate_1, w_gate_2, w_gate_3)
    w_up = (w_up_0, w_up_1, w_up_2, w_up_3)
    w_down = (w_down_0, w_down_1, w_down_2, w_down_3)
    home = (place.z, place.core, place.x)
    local = Local(local_sem)
    staged = []
    for whole, low, master, row, column in (
        (w_kv, 0, m_key, 192, 512),
        (w_kv, 128, m_value, 192, 640),
        (w_q, 0, m_query, 192, 0),
        (w_out, 0, m_output, 192, 768),
        (w_gate, 0, m_gate, 0, 0),
        (w_up, 0, m_up, 64, 0),
        (w_down, 0, m_down, 128, 0),
    ):
        width = master.shape[1]
        spot = f_sum.at[pl.ds(row, 64), pl.ds(column, width)]
        staged.append((whole, low, width, row, spot, local.copy(master, spot)))
    load_tokens = local.copy(in_tokens, tokens)
    load_back = local.copy(in_cotangent, cotangent)
    greet(place, PARTNERS)

    def place_own(entries):
        for whole, low, width, row, spot, copy in entries:
            local.done(copy)
            if isinstance(whole, tuple):
                for part in range(4):
                    cut = pl.ds(row, 64), pl.ds(part * 512, 512)
                    whole[part][(*home, slice(None), slice(None))] = narrow(f_sum[cut])
            else:
                whole[(*home, slice(None), slice(low, low + width))] = narrow(spot[...])

    wire = Wire(place, send_sem, recv_sem)
    pump = Course(FORWARD_COURSE)
    place_own(staged[:3])
    kv_ready = [
        pump.add(gather_chunk(wire, w_kv, 0, 128, "x")),
        pump.add(gather_chunk(wire, w_kv, 128, 128, "z")),
    ]
    ready = [
        pump.add(gather_chunk(wire, w_q, 0, 256, "x")),
        pump.add(gather_chunk(wire, w_q, 256, 256, "z")),
    ]
    pump.point()
    place_own(staged[3:])
    out_ready = [
        pump.add(gather_chunk(wire, w_out, 0, 256, "x")),
        pump.add(gather_chunk(wire, w_out, 256, 256, "z")),
    ]
    down_ready, feed_ready = [], []
    for part in range(4):
        flows = [
            pump.add(gather_chunk(wire, whole[part], 0, 512, ("x", "z")[(part + number) % 2]))
            for number, whole in enumerate((w_down, w_gate, w_up))
        ]
        down_ready.append(flows[0])
        feed_ready.append(flows)

    pump.point()
    local.done(load_tokens)
    for half in range(2):
        value = wide(tokens[half]).reshape(128, WIDTH)
        normed[half] = narrow(value * root_scale(value) * gains[0:1, :]).reshape(4, 32, WIDTH)
    transpose_into(flip, normed)
    flipped = local.copy(flip, out_n1_t)
    pump.point()
    spots = lax.broadcasted_iota(jnp.int32, (7, 32), 1)
    inverse = jnp.zeros((7, 32), jnp.int32)
    for block in range(32):
        inverse = jnp.where(owner_rows[:, block : block + 1] == spots, block, inverse)
    out_slots[...] = inverse
    ids = segments[...]
    start_one = jnp.sum(jnp.where(ids < 1, 1, 0), axis=1, keepdims=True)
    start_two = jnp.sum(jnp.where(ids < 2, 1, 0), axis=1, keepdims=True)

    def begins(at):
        return jnp.where(at >= start_two, start_two, jnp.where(at >= start_one, start_one, 0))

    at = place.x * 256 + lax.broadcasted_iota(jnp.int32, (256, 128), 0)
    angle = (at - begins(at)).astype(F32) * rates[...]
    tables[0] = jnp.cos(angle)
    tables[1] = jnp.sin(angle)
    local.copy(tables, out_tables)
    pump.point()
    pump.until(kv_ready)
    local.copy(w_kv, out_w_kv)

    lhs = normed[...].reshape(256, WIDTH)
    key_rows = times(lhs, natural_rows(w_kv, owners, 1, 0, 32, slice(0, 128)))
    kv[place.x, :, 0:128] = narrow(rotate(key_rows, tables[0], tables[1]))
    value_rows = times(lhs, natural_rows(w_kv, owners, 2, 0, 32, slice(128, 256)))
    kv[place.x, :, 128:256] = narrow(value_rows)
    shares = [wire.send(kv.at[place.x], kv.at[place.x], "x", step) for step in (1, -1, 2)]

    pump.point()

    def mask(index):
        half, block = lax.div(index, 4), lax.rem(index, 4)
        at = place.x * 256 + half * 128 + lax.broadcasted_iota(jnp.int32, (1, 128), 1)
        key_at = block * 256 + lax.broadcasted_iota(jnp.int32, (256, 128), 0)
        bias[half, pl.ds(pl.multiple_of(block * 256, 256), 256), :] = jnp.where(
            (key_at <= at) & (key_at >= begins(at)), 0.0, masked_score
        )

    loop(8, mask)
    pump.point()
    local.done(load_back, flipped)
    transpose_into(flip, cotangent)
    flipped = local.copy(flip, out_back_t)

    pump.until(ready)
    local.copy(w_q, out_w_q)
    pump.point()

    def query(slab):
        cut = columns(slab, 128)
        rows = times(normed[...].reshape(256, WIDTH), natural_rows(w_q, owners, 0, 0, 32, cut))
        q_out[:, cut] = narrow(rotate(rows, tables[0], tables[1]) * SCALE)

    loop(1, query)
    pump.point()
    loop(1, lambda slab: query(slab + 1))
    pump.point()
    loop(1, lambda slab: query(slab + 2))
    pump.point()
    loop(1, lambda slab: query(slab + 3))
    local.copy(q_out, out_q)
    q_t8[...] = jnp.zeros_like(q_t8)
    for slab in range(4):
        turned = narrow(wide(q_out[:, slab * 128 : slab * 128 + 128]).T)
        goal = slice(slab // 2 * 64, slab // 2 * 64 + 64)
        for half in range(2):
            here = slice(half * 128, half * 128 + 128)
            q_t8[half * 4 + slab, goal, 0:128] = turned[0:64, here]
            q_t8[half * 4 + slab, goal, 128:256] = turned[64:128, here]
    pump.point()
    for copy in shares:
        copy.wait_recv()
    local.copy(kv, out_kv)
    for block in range(4):
        v_t[:, block * 256 : block * 256 + 256] = narrow(wide(kv[block, :, 128:256]).T)

    def attend(index, slot):
        hidden_keys = bias[lax.div(index, 4)]
        scores = times(kv[:, :, 0:128].reshape(1024, 128), q_t8[index]) + jnp.concatenate(
            [hidden_keys, hidden_keys], axis=1
        )
        top = jnp.max(scores, axis=0, keepdims=True)
        raised = jnp.exp(scores - top)
        low = narrow(raised * (1.0 / jnp.sum(raised, axis=0, keepdims=True)))
        probs[slot] = low
        goal = pl.ds(pl.multiple_of(lax.div(lax.rem(index, 4), 2) * 64, 64), 64)
        o_t[index] = times(v_t[goal, :], low)

    kept = []

    def attend_group(group):
        if group > 1:
            local.done(kept[group - 2])
        slot = group % 2 * 2
        loop(2, lambda index: attend(index + 2 * group, index + slot))
        kept.append(local.copy(probs.at[pl.ds(slot, 2)], out_probs.at[pl.ds(group * 2, 2)]))

    def project_half(half):
        here = slice(half * 128, half * 128 + 128)
        for slab in range(4):
            value = o_t[half * 4 + slab]
            both = jnp.concatenate([value[:, 0:128], value[:, 128:256]], axis=0)
            attended[here, slab * 128 : slab * 128 + 128] = narrow(both.T)

        def project(part):
            rows = natural_rows(w_out, owners, 3, part * 4, 4, slice(None))
            normed[half, :, :, columns(part, 256)] = narrow(
                times(attended[here, :], rows, LAST)
            ).reshape(4, 32, 256)

        loop(4, project)
        pump.point()
        loop(4, lambda part: project(part + 4))

    def second_norm(half):
        mid = wide(tokens[half, place.y]) + ring_total(wire, "y", normed.at[half], far.at[half])
        mid_out[half] = mid
        normed_two[half, place.y] = narrow(mid * root_scale(mid) * gains[1:2, :])

    def feed_back(part, index):
        back = cotangent[...].reshape(256, WIDTH)
        rows = natural_rows(w_down[part], owners, 6, 0, 32, columns(index, 256))
        hidden[:, columns(index + part * 2, 256)] = narrow(times(back, rows))

    def feed_back_part(part):
        pump.until(down_ready[part : part + 1])
        loop(2, lambda index: feed_back(part, index))

    sums = [ring_sum(wire, "y", normed.at[h], near.at[h], far.at[h], 1) for h in range(2)]
    spreads = [ring_spread(wire, "y", normed_two.at[h], 1) for h in range(2)]
    attend_group(0)
    pump.point()
    attend_group(1)
    pump.point()
    pump.until(out_ready)
    local.copy(w_out, out_w_out)
    project_half(0)
    next(sums[0])
    pump.point()
    attend_group(2)
    pump.point()
    next(sums[0])
    attend_group(3)
    pump.point()
    project_half(1)
    next(sums[1])
    pump.point()
    next(sums[0], None)
    second_norm(0)
    next(spreads[0])
    pump.point()
    next(sums[1])
    pump.point()
    next(spreads[0])
    local.copy(attended, out_attended)
    pump.point()
    if EAGER > 0:
        feed_back_part(0)
    pump.point()
    next(sums[1], None)
    second_norm(1)
    next(spreads[1])
    local.copy(mid_out, out_mid)
    next(spreads[0], None)
    pump.point()
    if EAGER > 1:
        feed_back_part(1)
    next(spreads[1])
    pump.point()
    if EAGER > 2:
        feed_back_part(2)
    next(spreads[1], None)

    def feed(part, index):
        cut = columns(index + part * 2, 256)
        here = columns(index, 256)
        lhs = normed_two[...].reshape(256, WIDTH)
        gate = times(lhs, natural_rows(w_gate[part], owners, 4, 0, 32, here))
        up = times(lhs, natural_rows(w_up[part], owners, 5, 0, 32, here))
        d_hidden = wide(hidden[:, cut])
        sigmoid = jax.nn.sigmoid(gate)
        silu = gate * sigmoid
        hidden[:, cut] = narrow(silu * up)
        d_gate[:, cut] = narrow(d_hidden * up * sigmoid * (1.0 + gate * (1.0 - sigmoid)))
        d_up[:, cut] = narrow(d_hidden * silu)

    def project_feed(part):
        units = slice(part * 512, part * 512 + 512)

        def rows_of(whole, matrix, index):
            return natural_rows(whole[part], owners, matrix, index * 4, 4, slice(None))

        def tile(index):
            cut = columns(index, 256)
            down = times(hidden[:, units], rows_of(w_down, 6, index), LAST)
            back = times(
                jnp.concatenate([d_gate[:, units], d_up[:, units]], axis=1),
                jnp.concatenate([rows_of(w_gate, 4, index), rows_of(w_up, 5, index)], axis=1),
                LAST,
            )
            if part > 0:
                down = f_sum[:, cut] + down
                back = dn_sum[:, cut] + back
            if part < 3:
                f_sum[:, cut] = down
                dn_sum[:, cut] = back
            else:
                normed_two[:, :, :, cut] = narrow(down).reshape(2, 4, 32, 256)
                normed[:, :, :, cut] = narrow(back).reshape(2, 4, 32, 256)

        loop(4, tile)
        pump.point()
        loop(4, lambda index: tile(index + 4))

    for part in range(4):
        if part >= EAGER:
            feed_back_part(part)
        pump.until(feed_ready[part])
        loop(1, lambda index: feed(part, index))
        pump.point()
        loop(1, lambda index: feed(part, index + 1))
        pump.point()
        if part == 0:
            local.copy(normed_two, out_n2)
        if part == 3:
            wire.finish()
            local.finish()
            for source, target in ((hidden, out_hidden), (d_gate, out_d_gate), (d_up, out_d_up)):
                local.copy(source, target)
        project_feed(part)
        pump.point()
    local.copy(normed, out_dn)
    local.copy(normed_two, out_f)
    local.finish()


def forward(tokens, cotangent, segments, owners, gains, masters):
    def shape(*sizes, dtype=BF16):
        return jax.ShapeDtypeStruct(sizes, dtype)

    rates = jnp.asarray(np.tile(rope_frequencies(HEAD_SIZE), 4)[None, :])
    outs = [
        shape(4, 2, 4, 64, 512),
        shape(4, 2, 4, 64, 256),
        shape(4, 2, 4, 64, 512),
        shape(2, 32, WIDTH, dtype=F32),
        shape(32, 64, 256),
        shape(2, 4, 32, WIDTH),
        shape(32, 64, 256),
        shape(256, WIDTH),
        shape(256, WIDTH),
        shape(256, WIDTH),
        shape(2, 4, 32, WIDTH),
        shape(2, 4, 32, WIDTH),
        shape(8, 1024, 256),
        shape(256, 512),
        shape(4, 256, 256),
        shape(256, 512),
        shape(2, 256, 128, dtype=F32),
        shape(7, 32, dtype=jnp.int32),
    ]
    scratch = [
        pltpu.VMEM((2, 4, 32, WIDTH), BF16),
        pltpu.VMEM((2, 4, 32, WIDTH), BF16),
        pltpu.VMEM((4, 2, 4, 64, 512), BF16),
        pltpu.VMEM((4, 2, 4, 64, 256), BF16),
        pltpu.VMEM((4, 2, 4, 64, 512), BF16),
        *[pltpu.VMEM((4, 2, 4, 64, 512), BF16)] * 12,
        pltpu.VMEM((2, 32, WIDTH), F32),
        pltpu.VMEM((32, 64, 256), BF16),
        pltpu.VMEM((256, WIDTH), BF16),
        pltpu.VMEM((256, WIDTH), BF16),
        pltpu.VMEM((256, WIDTH), BF16),
        pltpu.VMEM((4, 1024, 256), BF16),
        pltpu.VMEM((256, 512), BF16),
        pltpu.VMEM((4, 256, 256), BF16),
        pltpu.VMEM((256, 512), BF16),
        pltpu.VMEM((2, 256, 128), F32),
        pltpu.VMEM((2, 4, 32, WIDTH), BF16),
        pltpu.VMEM((2, 4, 32, WIDTH), BF16),
        pltpu.VMEM((256, WIDTH), F32),
        pltpu.VMEM((256, WIDTH), F32),
        pltpu.VMEM((2, 2, 16, WIDTH), BF16),
        pltpu.VMEM((2, 2, 32, WIDTH), BF16),
        pltpu.VMEM((2, 1024, 128), F32),
        pltpu.VMEM((8, 128, 256), BF16),
        pltpu.VMEM((128, 1024), BF16),
        pltpu.VMEM((8, 64, 256), F32),
        pltpu.SemaphoreType.DMA((40,)),
        pltpu.SemaphoreType.DMA((240,)),
        pltpu.SemaphoreType.DMA((240,)),
    ]
    return pl.pallas_call(
        forward_body,
        out_shape=outs,
        in_specs=[ANYWHERE] * 2 + [IN_VMEM, IN_SMEM] + [IN_VMEM] * 3 + [ANYWHERE] * 7,
        out_specs=[ANYWHERE] * (len(outs) - 1) + [IN_VMEM],
        scratch_shapes=scratch,
        compiler_params=pltpu.CompilerParams(
            collective_id=1, has_side_effects=True, vmem_limit_bytes=VMEM_BYTES
        ),
        name="forward",
    )(
        tokens.reshape(2, 4, 32, WIDTH),
        cotangent.reshape(2, 4, 32, WIDTH),
        segments,
        owners,
        owners,
        gains,
        rates,
        *masters,
    )


DEPTH = 8
SIDES = (("x", 1), ("x", -1), ("z", 1), ("z", -1), ("core", 1))


def reduce_chunk(wire, fill, slot, buffers, credit, take, give, first, finish, gap):
    place = wire.place
    second = "z" if first == "x" else "x"
    own, other, core = place.at(first), place.at(second), place.core
    pieces, near, far, one, two = buffers
    if take:
        for side in range(5):
            pl.semaphore_wait(credit.at[side], 1)
    fill(slot)
    copies = [wire.send(slot.at[:, 1 - core], pieces, "core", 1)]
    yield 1
    copies[0].wait_recv()

    def add_pair(row):
        pieces[row] = pieces[row] + slot[row, core]

    loop(4, add_pair)
    wire.sent(copies[:1])

    def spot(line, place_in):
        return (line, place_in) if first == "z" else (place_in, line)

    before, after, facing = wrap(own - 1), wrap(own + 1), wrap(own + 2)
    right = wire.send(pieces.at[spot(facing, LOW)], near.at[0], first, 1)
    left = wire.send(pieces.at[spot(facing, HIGH)], near.at[1], first, -1)
    copies += [right, left]
    yield gap
    right.wait_recv()
    left.wait_recv()
    here = spot(after, LOW)
    pieces[here] = pieces[here] + near[0]
    here = spot(before, HIGH)
    pieces[here] = pieces[here] + near[1]
    right = wire.send(pieces.at[spot(after, FULL)], far.at[0], first, 1)
    left = wire.send(pieces.at[spot(before, FULL)], far.at[1], first, -1)
    copies += [right, left]
    yield gap
    right.wait_recv()
    left.wait_recv()
    here = spot(own, FULL)
    pieces[here] = narrow(wide(pieces[here]) + wide(far[0]) + wide(far[1]))
    before, after, facing = wrap(other - 1), wrap(other + 1), wrap(other + 2)
    low_rows, high_rows = pl.ds(0, 32), pl.ds(32, 32)
    right = wire.send(pieces.at[spot(own, facing) + (low_rows,)], one.at[0], second, 1)
    left = wire.send(pieces.at[spot(own, facing) + (high_rows,)], one.at[1], second, -1)
    copies += [right, left]
    yield 1
    right.wait_recv()
    left.wait_recv()
    here = spot(own, after) + (low_rows,)
    pieces[here] = pieces[here] + one[0]
    here = spot(own, before) + (high_rows,)
    pieces[here] = pieces[here] + one[1]
    right = wire.send(pieces.at[spot(own, after)], two.at[0], second, 1)
    left = wire.send(pieces.at[spot(own, before)], two.at[1], second, -1)
    copies += [right, left]
    yield 1
    right.wait_recv()
    left.wait_recv()
    finish(wide(pieces[spot(own, other)]) + wide(two[0]) + wide(two[1]))
    wire.sent(copies[1:])
    if give:
        for side, (axis, step) in enumerate(SIDES):
            back = SIDES.index((axis, -step)) if axis != "core" else 4
            pl.semaphore_signal(
                credit.at[back], inc=1, device_id=place.toward(axis, step), device_id_type=MESH
            )


SLOTS = 2
TURNS = 15
FEED_FIRST, FEED_SECOND = 9, 12
BACKWARD_COURSE = (
    (),
    (0, 1),
    (),
    (0, 2, 1, 3),
    (2, 0, 4, 3),
    (1, 5, 2, 4),
    (6, 3, 5),
    (),
    (0, 6),
    (1, 2),
    (4,),
    (0, 2, 3, 5, 6),
    (0, 1, 4),
    (3, 6, 1, 2, 7, 4, 5, 8),
    (3, 7, 4, 6, 5, 12, 8, 9),
    (),
    (7, 12),
    (5, 6, 9, 8, 10, 11, 12),
    (),
    (7, 10, 11),
    (8, 9, 13, 14),
    (8, 12, 7, 13, 14),
    (11, 10, 7, 15, 9),
    (8, 13, 15, 16),
    (16,),
    (12,),
    (14, 17, 11, 9, 17, 10, 16, 13, 15, 12, 9, 17, 10, 14, 11, 15, 16, 17, 13, 10, 11, 14, 15, 16, 17, 13, 15, 14, 17, 16),
)


def backward_body(
    in_tokens,
    in_cotangent,
    owners,
    slots,
    gains,
    in_w_q,
    in_w_kv,
    in_w_out,
    in_mid,
    in_n1_t,
    in_n2,
    in_back_t,
    in_hidden,
    in_d_gate,
    in_d_up,
    dn_in,
    f_in,
    in_probs,
    in_queries,
    in_kv,
    in_attended,
    in_tables,
    out_output,
    out_grad_low,
    out_query,
    out_key,
    out_value,
    out_output_grad,
    out_gate,
    out_up,
    out_down,
    g_gains,
    tokens,
    cotangent,
    output,
    grad_low,
    g_query,
    g_key,
    g_value,
    g_output,
    g_gate,
    g_up,
    g_down,
    w_qkv,
    w_out,
    mid,
    n1_t,
    n2_t,
    back_t,
    hidden,
    d_gate,
    d_up,
    probs,
    queries,
    kv,
    attended,
    tables,
    pieces,
    near,
    far,
    one,
    two,
    fills,
    gain_fill,
    dn_mine,
    dn_near,
    dn_far,
    f_mine,
    f_near,
    f_far,
    n_mine,
    n_near,
    n_far,
    kv_mine,
    kv_near,
    kv_far,
    da,
    da_t,
    d_mid,
    d_t8,
    d_8,
    q_8,
    k_t,
    dq_t,
    dk_sum,
    dv_sum,
    d_query,
    d_key,
    d_value,
    gain_rows,
    gain_all,
    scales,
    credit,
    local_sem,
    send_sem,
    recv_sem,
):
    place = Place()
    local = Local(local_sem)
    load_dn = local.copy(dn_in, dn_mine)
    load_down = [local.copy(in_back_t, back_t), local.copy(in_hidden, hidden)]
    load_n2 = local.copy(in_n2, da)
    load_gate = [local.copy(in_d_gate, d_gate)]
    load_up = [local.copy(in_d_up, d_up)]
    load_mid = [
        local.copy(in_cotangent, cotangent),
        local.copy(in_mid, mid),
        local.copy(in_w_out, w_out),
    ]
    load_heads = [
        local.copy(in_kv, kv),
        local.copy(in_queries, queries),
        local.copy(in_probs.at[pl.ds(0, 2)], probs.at[pl.ds(0, 2)]),
        local.copy(in_probs.at[pl.ds(2, 2)], probs.at[pl.ds(2, 2)]),
    ]
    load_f = local.copy(f_in, f_mine)
    load_out = [local.copy(in_attended, attended)]
    load_late = [
        local.copy(in_tokens, tokens),
        local.copy(in_tables, tables),
        local.copy(in_w_q, w_qkv.at[:, :, :, :, pl.ds(0, 512)]),
        local.copy(in_w_kv, w_qkv.at[:, :, :, :, pl.ds(512, 256)]),
        local.copy(in_n1_t, n1_t),
    ]
    greet(place, PARTNERS)
    wire = Wire(place, send_sem, recv_sem)
    pump = Course(BACKWARD_COURSE)
    def chunk_flow(turn, slot, low, width, fill, finish, take, give, first, gap):
        size = pl.ds(low, width)
        buffers = [
            pieces.at[turn, :, :, :, size],
            near.at[turn, :, :, :, size],
            far.at[turn, :, :, :, size],
            one.at[turn, :, :, size],
            two.at[turn, :, :, size],
        ]
        space = gain_fill if slot is None else fills.at[slot, :, :, :, :, size]
        return reduce_chunk(wire, fill, space, buffers, credit, take, give, first, finish, gap)

    def product(matrix, left, right, low, width, loads=()):
        def fill(slot):
            local.done(*loads)

            def rows(index):
                lhs = jnp.concatenate(
                    [left[slots[matrix, index * 8 + step]] for step in range(8)], axis=0
                )
                slot[index] = narrow(times(lhs, right[:, pl.ds(low, width)])).reshape(
                    2, 4, 64, width
                )

            loop(4, rows)

        return fill

    def keep(target, out, low, width):
        def finish(value):
            cut = pl.ds(low, width)
            target[:, cut] = value
            local.copy(target.at[:, cut], out.at[:, cut])

        return finish

    def add_feed(turn, matrix, left, right, target, out, low, loads=()):
        flow = chunk_flow(
            turn % DEPTH,
            turn % SLOTS,
            0,
            512,
            product(matrix, left, right, low, 512, loads),
            keep(target, out, low, 512),
            turn >= DEPTH,
            turn < TURNS - DEPTH,
            ("x", "z")[turn // 2 % 2],
            1,
        )
        pump.add(flow, turn)

    def add_rest(turn, parts):
        for matrix, right, target, out, low, width, at, first in parts:
            flow = chunk_flow(
                turn % DEPTH,
                turn % SLOTS,
                at,
                width,
                product(matrix, n1_t, right, low, width),
                keep(target, out, low, width),
                at == 0,
                turn < TURNS - DEPTH,
                first,
                1,
            )
            pump.add(flow, turn)

    turn_of = {}
    for number in range(12):
        turn_of[number] = number + (number >= FEED_FIRST) + (number >= FEED_SECOND)
    out_turn, query_turn = FEED_FIRST, FEED_SECOND + 1
    for part in range(4):
        loads = () if part else load_down
        add_feed(turn_of[part], 6, back_t, hidden, g_down, out_down, part * 512, loads)
    local.done(load_dn)
    def halves(mine, near_rows, far_rows, parts):
        return [
            ring_sum(wire, "y", mine.at[h], near_rows.at[h], far_rows.at[h], parts)
            for h in range(2)
        ]

    def norm_back(half):
        mine = mid[half]
        scale = root_scale(mine)
        hat = mine * scale
        total = ring_total(wire, "y", dn_mine.at[half], dn_far.at[half])
        gained = jnp.sum(total * hat, axis=0, keepdims=True)
        gain_rows[1:2, :] = gained if half == 0 else gain_rows[1:2, :] + gained
        scaled = total * gains[1:2, :]
        value = wide(cotangent[half, place.y]) + scale * (
            scaled - hat * jnp.mean(scaled * hat, axis=-1, keepdims=True)
        )
        d_mid[half] = value
        da[half, place.y] = narrow(value)

    lane = lax.broadcasted_iota(jnp.int32, (128, 128), 1)

    def heads_of(half):
        here = slice(half * 128, half * 128 + 128)

        def attended_back(slab):
            cut = columns(slab, 256)
            rows = times(
                da[half].reshape(128, WIDTH), natural_rows(w_out, owners, 3, 0, 32, cut)
            )
            d_query[here, cut] = narrow(rows)

        loop(2, attended_back)
        for slab in range(4):
            goal = slab // 2
            cut = slice(slab * 128, slab * 128 + 128)
            index = half * 4 + slab
            for source, rows in ((queries, q_8), (d_query, d_8)):
                value = wide(source[here, cut])
                for side in range(2):
                    moved = value if side == goal else pltpu.roll(value, 64, 1)
                    rows[index, side * 128 : side * 128 + 128, :] = narrow(
                        jnp.where((lane < 64) == (goal == 0), moved, 0.0)
                    )
            turned = narrow(wide(d_query[here, cut]).T)
            d_t8[index, goal * 64 : goal * 64 + 64, 0:128] = turned[0:64]
            d_t8[index, goal * 64 : goal * 64 + 64, 128:256] = turned[64:128]

    sums = halves(dn_mine, dn_near, dn_far, 1)
    spreads = [ring_spread(wire, "y", da.at[h], 1) for h in range(2)]
    next(sums[0])
    next(sums[1])
    pump.point()
    local.done(load_n2)
    transpose_into(n2_t, da)
    for part in range(4):
        cut = part * 512
        loads = () if part else load_gate
        add_feed(turn_of[4 + 2 * part], 4, n2_t, d_gate, g_gate, out_gate, cut, loads)
        loads = () if part else load_up
        add_feed(turn_of[5 + 2 * part], 5, n2_t, d_up, g_up, out_up, cut, loads)
    pump.point()
    next(sums[0])
    pump.point()
    next(sums[1])
    local.done(*load_mid)
    d_t8[...] = jnp.zeros_like(d_t8)
    dk_sum[...] = jnp.zeros_like(dk_sum)
    dv_sum[...] = jnp.zeros_like(dv_sum)
    pump.point()
    next(sums[0], None)
    norm_back(0)
    next(spreads[0])
    pump.point()
    next(sums[1], None)
    norm_back(1)
    next(spreads[1])
    local.done(*load_heads[:2])
    for block in range(4):
        k_t[:, block * 256 : block * 256 + 256] = narrow(wide(kv[block, :, 0:128]).T)
    pump.point()
    next(spreads[0])
    pump.point()
    next(spreads[1])
    pump.point()
    next(spreads[0], None)
    heads_of(0)
    pump.point()

    def attend_back(index, slot):
        low = probs[slot]
        prob = wide(low)
        d_prob = times(kv[:, :, 128:256].reshape(1024, 128), d_t8[index])
        kept = prob * d_prob
        d_score = narrow(kept - prob * jnp.sum(kept, axis=0, keepdims=True))
        goal = pl.ds(pl.multiple_of(lax.div(lax.rem(index, 4), 2) * 64, 64), 64)
        dq_t[index] = times(k_t[goal, :], d_score)
        dv_sum[...] += times(low, d_8[index])
        dk_sum[...] += times(d_score, q_8[index])

    coming = load_heads[2:]

    def attend_group(group):
        slot = group % 2 * 2
        local.done(coming[group % 2])
        loop(2, lambda index: attend_back(index + 2 * group, index + slot))
        if group < 2:
            here = pl.ds(slot, 2)
            coming[group % 2] = local.copy(in_probs.at[pl.ds(group * 2 + 4, 2)], probs.at[here])

    attend_group(0)
    pump.point()
    attend_group(1)
    pump.point()
    next(spreads[1], None)
    heads_of(1)
    local.done(load_f)
    f_flows = halves(f_mine, f_near, f_far, 1)
    for flow in f_flows:
        next(flow)
    transpose_into(da_t, da)
    add_feed(out_turn, 3, da_t, attended, g_output, out_output_grad, 0, load_out)
    pump.point()
    attend_group(2)
    for flow in f_flows:
        next(flow)
    pump.point()
    attend_group(3)
    kv_mine[:, :, 0:128] = narrow(dk_sum[...]).reshape(4, 256, 128)
    kv_mine[:, :, 128:256] = narrow(dv_sum[...]).reshape(4, 256, 128)
    kv_flow = ring_sum(wire, "x", kv_mine, kv_near, kv_far, 1)
    next(kv_flow)
    local.done(*load_late)
    for slab in range(4):
        cut = slice(slab * 128, slab * 128 + 128)
        for half in range(2):
            here = slice(half * 128, half * 128 + 128)
            value = dq_t[half * 4 + slab]
            both = jnp.concatenate([value[:, 0:128], value[:, 128:256]], axis=0).T * SCALE
            d_query[here, cut] = narrow(rotate_back(both, tables[0, here], tables[1, here]))
    add_rest(
        query_turn,
        (
            (0, d_query, g_query, out_query, 0, 256, 0, "x"),
            (0, d_query, g_query, out_query, 256, 256, 256, "z"),
        ),
    )
    pump.point()
    next(kv_flow)
    for half in range(2):
        next(f_flows[half], None)
        output[half, place.y] = narrow(
            mid[half] + ring_total(wire, "y", f_mine.at[half], f_far.at[half])
        )
    out_flows = [ring_spread(wire, "y", output.at[h], 1) for h in range(2)]
    for flow in out_flows:
        next(flow)
    for half in range(2):
        value = wide(tokens[half]).reshape(128, WIDTH)
        scales[half] = jnp.broadcast_to(root_scale(value), (128, 128))
    pump.point()
    for _ in kv_flow:
        pass
    total = ring_total(wire, "x", kv_mine, kv_far)
    d_key[...] = narrow(rotate_back(total[:, 0:128], tables[0], tables[1]))
    d_value[...] = narrow(total[:, 128:256])
    add_rest(
        TURNS - 1,
        (
            (1, d_key, g_key, out_key, 0, 128, 0, "x"),
            (2, d_value, g_value, out_value, 0, 128, 128, "z"),
        ),
    )
    pump.point()

    def project_back(index):
        cut = columns(index, 256)
        first = index * 4
        rows = [
            natural_rows(w_qkv, owners, matrix, first, 4, here)
            for matrix, here in enumerate((slice(0, 512), slice(512, 640), slice(640, 768)))
        ]
        part = times(
            jnp.concatenate([d_query[...], d_key[...], d_value[...]], axis=1),
            jnp.concatenate(rows, axis=1),
            LAST,
        )
        n_mine[:, :, :, cut] = narrow(part).reshape(2, 4, 32, 256)
        hat = wide(tokens[:, :, :, cut]).reshape(256, 256) * scales[:, :, 0:1].reshape(256, 1)
        gain_rows[0:1, cut] = jnp.sum(part * hat, axis=0, keepdims=True)

    n_flows = halves(n_mine, n_near, n_far, 2)
    loop(2, project_back)
    pump.point()
    loop(2, lambda index: project_back(index + 2))
    for flow in n_flows:
        next(flow)
    pump.point()
    loop(2, lambda index: project_back(index + 4))
    pump.point()
    loop(2, lambda index: project_back(index + 6))
    for flow in n_flows:
        next(flow)
    for flow in out_flows:
        next(flow)

    def gain_chunk(slot):
        slot[...] = jnp.zeros_like(slot)
        for block in range(32):
            low = block // 2 * 128
            slot[block // 8, block // 4 % 2, block % 4, 0:2, :] = narrow(
                gain_rows[0:2, low : low + 128]
            )

    def gain_finish(value):
        gain_all[place.y] = value[0:8]

    gain_flow = chunk_flow(
        (TURNS - 1) % DEPTH, None, 256, 128, gain_chunk, gain_finish, False, False, "x", 1
    )
    pump.add(gain_flow, TURNS)
    pump.point()
    for flow in n_flows:
        next(flow)
    for flow in out_flows:
        next(flow, None)
    local.copy(output, out_output)
    spreads = [ring_spread(wire, "y", grad_low.at[h], 1) for h in range(2)]
    for half in range(2):
        pump.point()
        next(n_flows[half], None)
        value = wide(tokens[half, place.y])
        scale = root_scale(value)
        hat = value * scale
        total = ring_total(wire, "y", n_mine.at[half], n_far.at[half])
        scaled = total * gains[0:1, :]
        grad_low[half, place.y] = narrow(
            d_mid[half]
            + scale * (scaled - hat * jnp.mean(scaled * hat, axis=-1, keepdims=True))
        )
        next(spreads[half])
    for flow in spreads:
        pump.point()
        next(flow)
    for flow in spreads:
        pump.point()
        next(flow, None)
    local.copy(grad_low, out_grad_low)
    pump.until(tuple(range(len(pump.flows))))
    shares = [
        wire.send(gain_all.at[place.y], gain_all.at[place.y], "y", step) for step in (1, -1, 2)
    ]
    for copy in shares:
        copy.wait_recv()
    g_gains[...] = gain_all[0] + gain_all[1] + gain_all[2] + gain_all[3]
    wire.finish()
    local.finish()


def backward(tokens, cotangent, owners, gains, kept):
    def shape(*sizes, dtype=BF16):
        return jax.ShapeDtypeStruct(sizes, dtype)

    *kept, slots = kept
    outs = [
        shape(2, 4, 32, WIDTH),
        shape(2, 4, 32, WIDTH),
        shape(64, 512, dtype=F32),
        shape(64, 128, dtype=F32),
        shape(64, 128, dtype=F32),
        shape(64, 512, dtype=F32),
        shape(64, 2048, dtype=F32),
        shape(64, 2048, dtype=F32),
        shape(64, 2048, dtype=F32),
        shape(8, 128, dtype=F32),
    ]
    scratch = [
        *[pltpu.VMEM((2, 4, 32, WIDTH), BF16)] * 4,
        *[pltpu.VMEM(out.shape, F32) for out in outs[2:9]],
        pltpu.VMEM((4, 2, 4, 64, 768), BF16),
        pltpu.VMEM((4, 2, 4, 64, 512), BF16),
        pltpu.VMEM((2, 32, WIDTH), F32),
        pltpu.VMEM((32, 64, 256), BF16),
        pltpu.VMEM((32, 64, 256), BF16),
        pltpu.VMEM((32, 64, 256), BF16),
        pltpu.VMEM((256, WIDTH), BF16),
        pltpu.VMEM((256, WIDTH), BF16),
        pltpu.VMEM((256, WIDTH), BF16),
        pltpu.VMEM((4, 1024, 256), BF16),
        pltpu.VMEM((256, 512), BF16),
        pltpu.VMEM((4, 256, 256), BF16),
        pltpu.VMEM((256, 512), BF16),
        pltpu.VMEM((2, 256, 128), F32),
        pltpu.VMEM((DEPTH, 4, 4, 64, 512), BF16),
        pltpu.VMEM((DEPTH, 2, 2, 64, 512), BF16),
        pltpu.VMEM((DEPTH, 2, 4, 64, 512), BF16),
        pltpu.VMEM((DEPTH, 2, 32, 512), BF16),
        pltpu.VMEM((DEPTH, 2, 64, 512), BF16),
        pltpu.VMEM((SLOTS, 4, 2, 4, 64, 512), BF16),
        pltpu.VMEM((4, 2, 4, 64, 128), BF16),
        *[
            pltpu.VMEM(sizes, BF16)
            for sizes in ((2, 4, 32, WIDTH), (2, 2, 16, WIDTH), (2, 2, 32, WIDTH)) * 3
        ],
        pltpu.VMEM((4, 256, 256), BF16),
        pltpu.VMEM((2, 128, 256), BF16),
        pltpu.VMEM((2, 256, 256), BF16),
        pltpu.VMEM((2, 4, 32, WIDTH), BF16),
        pltpu.VMEM((32, 64, 256), BF16),
        pltpu.VMEM((2, 32, WIDTH), F32),
        pltpu.VMEM((8, 128, 256), BF16),
        pltpu.VMEM((8, 256, 128), BF16),
        pltpu.VMEM((8, 256, 128), BF16),
        pltpu.VMEM((128, 1024), BF16),
        pltpu.VMEM((8, 64, 256), F32),
        pltpu.VMEM((1024, 128), F32),
        pltpu.VMEM((1024, 128), F32),
        pltpu.VMEM((256, 512), BF16),
        pltpu.VMEM((256, 128), BF16),
        pltpu.VMEM((256, 128), BF16),
        pltpu.VMEM((8, WIDTH), F32),
        pltpu.VMEM((4, 8, 128), F32),
        pltpu.VMEM((2, 128, 128), F32),
        pltpu.SemaphoreType.REGULAR((5,)),
        pltpu.SemaphoreType.DMA((64,)),
        pltpu.SemaphoreType.DMA((240,)),
        pltpu.SemaphoreType.DMA((240,)),
    ]
    specs = [ANYWHERE, ANYWHERE, IN_SMEM, IN_SMEM, IN_VMEM] + [ANYWHERE] * len(kept)
    return pl.pallas_call(
        backward_body,
        out_shape=outs,
        in_specs=specs,
        out_specs=[ANYWHERE] * 9 + [IN_VMEM],
        scratch_shapes=scratch,
        compiler_params=pltpu.CompilerParams(
            collective_id=2, has_side_effects=True, vmem_limit_bytes=VMEM_BYTES
        ),
        name="backward",
    )(
        tokens.reshape(2, 4, 32, WIDTH),
        cotangent.reshape(2, 4, 32, WIDTH),
        owners,
        slots,
        gains,
        *kept,
    )


def split_dot(left, right, contract=((1,), (0,))):
    high_left, high_right = narrow(left), narrow(right)
    low_left = narrow(left - wide(high_left))
    low_right = narrow(right - wide(high_right))
    return (
        times(high_left, high_right, contract)
        + times(high_left, low_right, contract)
        + times(low_left, high_right, contract)
    )


def update_body(count, *refs):
    in_output, in_grad, gains, gain_moments, gain_grad = refs[:5]
    ins, refs = refs[5 : 5 + 3 * count], refs[5 + 3 * count :]
    out_output, out_grad, new_gains, new_gain_moments = refs[:4]
    outs, refs = refs[4 : 4 + 2 * count], refs[4 + 2 * count :]
    output, grad_low, grad_wide, copy_sem = refs[0], refs[1], refs[2], refs[-1]
    space, directions = refs[3 : 3 + 3 * count], refs[3 + 3 * count : 3 + 4 * count]
    masters, moments, grads = space[:count], space[count : 2 * count], space[2 * count :]
    local = Local(copy_sem)
    order = sorted(range(count), key=lambda number: -ins[number].shape[1])
    loads = {}
    for number in order:
        loads[number] = [
            local.copy(ins[2 * count + number], grads[number]),
            local.copy(ins[count + number], moments[number]),
        ]
    load_grad = local.copy(in_grad, grad_low)
    load_output = local.copy(in_output, output)
    load_masters = [local.copy(ins[number], masters[number]) for number in range(count)]
    first, second, third = newton_coeffs
    grams = [None] * count
    for number in order:
        local.done(*loads[number])
        grad = grads[number][...]
        renewed = momentum_decay * moments[number][...] + grad
        moments[number][...] = renewed
        local.copy(moments[number], outs[count + number])
        direction = grad + momentum_decay * renewed
        direction = direction * (1.0 / (jnp.sqrt(jnp.sum(direction * direction)) + 1e-07))
        directions[number][...] = direction
        grams[number] = split_dot(direction, direction, LAST)
    local.done(load_output, load_grad)
    local.copy(output, out_output)
    for half in range(2):
        grad_wide[half * 128 : half * 128 + 128, :] = wide(grad_low[half]).reshape(128, WIDTH)
    local.copy(grad_wide, out_grad)
    spot = lax.axis_index("dp") * 4 + lax.axis_index("ctx")
    odd = lax.rem(spot, 2) == 1

    def half(value):
        return jnp.where(odd, pltpu.roll(value, 64, 1), value)[:, 0:64]

    grad = half(gain_grad[...])[0:2]
    slab = gains[:, columns(lax.div(spot, 2), 128)]
    renewed = momentum_decay * gain_moments[...] + grad
    new_gain_moments[...] = renewed
    new_gains[...] = half(jnp.concatenate([slab] * 4, axis=0))[0:2] - gain_rate * (
        grad + momentum_decay * renewed
    )
    factors = [None] * count
    diagonal = lax.broadcasted_iota(jnp.int32, (64, 64), 0) == lax.broadcasted_iota(
        jnp.int32, (64, 64), 1
    )
    for sweep in range(5):
        squares = [split_dot(gram, gram) for gram in grams]
        steps = [
            jnp.where(diagonal, first, 0.0) + second * gram + third * square
            for gram, square in zip(grams, squares)
        ]
        if sweep == 0:
            factors = steps
            part = [split_dot(step, gram) for step, gram in zip(steps, grams)]
        elif sweep < 4:
            both = [
                split_dot(step, jnp.concatenate([gram, factor], axis=1))
                for step, gram, factor in zip(steps, grams, factors)
            ]
            part = [value[:, 0:64] for value in both]
            factors = [value[:, 64:128] for value in both]
        else:
            factors = [split_dot(step, factor) for step, factor in zip(steps, factors)]
        if sweep < 4:
            grams = [split_dot(piece, step) for piece, step in zip(part, steps)]
    local.done(*load_masters)
    for number in order:
        scale = learning_rate * 0.2 * math.sqrt(max(64, masters[number].shape[1]))
        update = split_dot(factors[number], directions[number][...])
        masters[number][...] = (
            masters[number][...] * (1.0 - learning_rate * weight_decay) - scale * update
        )
        local.copy(masters[number], outs[number])
    local.finish()


def update_blocks(output, grad_low, gains, gain_moments, gain_grad, masters, moments, grads):
    count = len(masters)
    shapes = [jax.ShapeDtypeStruct(master.shape, F32) for master in masters]
    results = pl.pallas_call(
        lambda *refs: update_body(count, *refs),
        out_shape=[
            jax.ShapeDtypeStruct((256, WIDTH), BF16),
            jax.ShapeDtypeStruct((256, WIDTH), F32),
            jax.ShapeDtypeStruct(gain_moments.shape, F32),
            jax.ShapeDtypeStruct(gain_moments.shape, F32),
        ]
        + shapes
        + shapes,
        in_specs=[ANYWHERE] * 2 + [IN_VMEM] * 3 + [ANYWHERE] * (3 * count),
        out_specs=[ANYWHERE] * 2 + [IN_VMEM] * 2 + [ANYWHERE] * (2 * count),
        scratch_shapes=[
            pltpu.VMEM((256, WIDTH), BF16),
            pltpu.VMEM((2, 4, 32, WIDTH), BF16),
            pltpu.VMEM((256, WIDTH), F32),
        ]
        + [pltpu.VMEM(master.shape, F32) for master in masters] * 4
        + [pltpu.SemaphoreType.DMA((5 * count + 4,))],
        compiler_params=pltpu.CompilerParams(vmem_limit_bytes=VMEM_BYTES),
        name="update_blocks",
    )(
        output.reshape(256, WIDTH),
        grad_low,
        gains,
        gain_moments,
        gain_grad,
        *masters,
        *moments,
        *grads,
    )
    return results[:4], results[4 : 4 + count], results[4 + count :]


def on_device(
    tokens,
    cotangent,
    segments,
    owners,
    gains,
    gain_moments,
    query_master,
    key_master_blocks,
    value_master_blocks,
    output_master,
    gate_master,
    up_master,
    down_master,
    query_moment,
    key_momentum,
    value_momentum,
    output_moment,
    gate_moment,
    up_moment,
    down_moment,
):
    masters = (
        query_master,
        key_master_blocks,
        value_master_blocks,
        output_master,
        gate_master,
        up_master,
        down_master,
    )
    moments = (
        query_moment,
        key_momentum,
        value_momentum,
        output_moment,
        gate_moment,
        up_moment,
        down_moment,
    )
    kept = forward(tokens, cotangent, segments, owners, gains, masters)
    output, grad_low, *grads, gain_grad = backward(tokens, cotangent, owners, gains, kept)
    firsts, new_masters, new_moments = update_blocks(
        output, grad_low, gains, gain_moments, gain_grad, masters, moments, grads
    )
    return tuple(firsts[:2]) + tuple(new_masters) + tuple(new_moments) + tuple(firsts[2:])


def solution(mesh):
    return jax.shard_map(
        on_device,
        mesh=mesh,
        in_specs=(
            P(("dp", "ctx"), None),
            P(("dp", "ctx"), None),
            P("dp", None),
            P(),
            P(),
            P(None, ("dp", "ctx")),
            P(("dp", "ctx"), "tensor"),
            P(("dp", "ctx"), "tensor"),
            P(("dp", "ctx"), "tensor"),
            P(("dp", "ctx"), "tensor"),
            P(("dp", "ctx"), "tensor"),
            P(("dp", "ctx"), "tensor"),
            P(("dp", "ctx"), "tensor"),
            P(("dp", "ctx"), "tensor"),
            P(("dp", "ctx"), "tensor"),
            P(("dp", "ctx"), "tensor"),
            P(("dp", "ctx"), "tensor"),
            P(("dp", "ctx"), "tensor"),
            P(("dp", "ctx"), "tensor"),
            P(("dp", "ctx"), "tensor"),
        ),
        out_specs=(
            P(("dp", "ctx"), None),
            P(("dp", "ctx"), None),
            P(("dp", "ctx"), "tensor"),
            P(("dp", "ctx"), "tensor"),
            P(("dp", "ctx"), "tensor"),
            P(("dp", "ctx"), "tensor"),
            P(("dp", "ctx"), "tensor"),
            P(("dp", "ctx"), "tensor"),
            P(("dp", "ctx"), "tensor"),
            P(("dp", "ctx"), "tensor"),
            P(("dp", "ctx"), "tensor"),
            P(("dp", "ctx"), "tensor"),
            P(("dp", "ctx"), "tensor"),
            P(("dp", "ctx"), "tensor"),
            P(("dp", "ctx"), "tensor"),
            P(("dp", "ctx"), "tensor"),
            P(None, ("dp", "ctx")),
            P(None, ("dp", "ctx")),
        ),
        check_vma=False,
    )
```

```python
import math

import jax
import jax.numpy as jnp
import numpy as np
from jax import lax
from jax.experimental import pallas as pl
from jax.experimental.pallas import tpu as pltpu
from jax.sharding import PartitionSpec as P

HEAD_SIZE = 64
WIDTH = 2048
SCALE = HEAD_SIZE ** (-0.5)

norm_epsilon = 1e-05
rope_base = 500000.0
momentum_decay = 0.95
learning_rate = 0.1
weight_decay = 0.01
gain_rate = 0.001
newton_coeffs = (3.4445, -4.775, 2.0315)
masked_score = -1e30

MESH = pl.DeviceIdType.MESH
VMEM_BYTES = 62 * 1024 * 1024
BF16, F32 = jnp.bfloat16, jnp.float32
ANYWHERE = pl.BlockSpec(memory_space=pl.ANY)
IN_VMEM = pl.BlockSpec(memory_space=pltpu.VMEM)
IN_SMEM = pl.BlockSpec(memory_space=pltpu.SMEM)


def rope_frequencies(head_dim):
    even = np.arange(0, head_dim, 2, dtype=np.float32)
    base_rates = np.float32(1.0) / np.float32(rope_base) ** (even / np.float32(head_dim))
    wavelength = np.float32(2.0 * math.pi) / base_rates
    smooth = (np.float32(8192.0) / wavelength - np.float32(1.0)) / np.float32(3.0)
    low_rates = base_rates / np.float32(32.0)
    blended = (np.float32(1.0) - smooth) * low_rates + smooth * base_rates
    return np.where(
        wavelength < 2048.0, base_rates, np.where(wavelength > 8192.0, low_rates, blended)
    ).astype(np.float32)


def wide(value):
    return value.astype(F32)


def narrow(value):
    return value.astype(BF16)


def times(left, right, contract=((1,), (0,))):
    return lax.dot_general(left, right, (contract, ((), ())), preferred_element_type=F32)


LAST = ((1,), (1,))


def wrap(value):
    return lax.rem(value + 4, 4)


class Place:
    def __init__(self):
        self.dp = lax.axis_index("dp")
        self.x = lax.axis_index("ctx")
        self.y = lax.axis_index("tensor")
        self.z = lax.div(self.dp, 2)
        self.core = lax.rem(self.dp, 2)
        self.known = {}

    def at(self, axis):
        return {"x": self.x, "y": self.y, "z": self.z}[axis]

    def toward(self, axis, step):
        if (axis, step) not in self.known:
            self.known[axis, step] = self.reach(axis, step)
        return self.known[axis, step]

    def reach(self, axis, step):
        if axis == "x":
            return (self.dp, wrap(self.x + step), self.y)
        if axis == "y":
            return (self.dp, self.x, wrap(self.y + step))
        if axis == "z":
            return (wrap(self.z + step) * 2 + self.core, self.x, self.y)
        return (self.z * 2 + 1 - self.core, self.x, self.y)


class Wire:
    def __init__(self, place, send_sem, recv_sem):
        self.place, self.send_sem, self.recv_sem = place, send_sem, recv_sem
        self.count, self.open = 0, []

    def send(self, source, target, axis, step):
        copy = pltpu.make_async_remote_copy(
            src_ref=source,
            dst_ref=target,
            send_sem=self.send_sem.at[self.count],
            recv_sem=self.recv_sem.at[self.count],
            device_id=self.place.toward(axis, step),
            device_id_type=MESH,
        )
        copy.start()
        self.count += 1
        self.open.append(copy)
        return copy

    def sent(self, copies):
        for copy in copies:
            copy.wait_send()
            self.open = [other for other in self.open if other is not copy]

    def finish(self):
        for copy in self.open:
            copy.wait_send()


class Local:
    def __init__(self, sem):
        self.sem, self.count, self.open = sem, 0, []

    def copy(self, source, target):
        copy = pltpu.make_async_copy(source, target, self.sem.at[self.count])
        copy.start()
        self.count += 1
        self.open.append(copy)
        return copy

    def done(self, *copies):
        for copy in copies:
            copy.wait()
            self.open = [other for other in self.open if other is not copy]

    def finish(self):
        self.done(*self.open)


def greet(place, partners):
    barrier = pltpu.get_barrier_semaphore()
    for axis, step in partners:
        pl.semaphore_signal(
            barrier, inc=1, device_id=place.toward(axis, step), device_id_type=MESH
        )
    pl.semaphore_wait(barrier, len(partners))


PARTNERS = (
    ("x", 1),
    ("x", -1),
    ("z", 1),
    ("z", -1),
    ("core", 1),
    ("y", 1),
    ("y", -1),
    ("x", 2),
    ("y", 2),
)


class Course:
    def __init__(self, table):
        self.table, self.count, self.flows = table, 0, []

    def add(self, flow, turn=0):
        self.flows.append(flow)
        return len(self.flows) - 1

    def step(self, number):
        if next(self.flows[number], None) is None:
            self.flows[number] = iter(())

    def point(self):
        if self.count < len(self.table):
            for number in self.table[self.count]:
                self.step(number)
        self.count += 1

    def until(self, numbers):
        self.point()
        for number in numbers:
            for _ in self.flows[number]:
                pass
            self.flows[number] = iter(())


FULL, LOW, HIGH = pl.ds(0, 4), pl.ds(0, 2), pl.ds(2, 2)


def gather_chunk(wire, whole, low, width, first, gaps=(1, 1, 1, 1, 1)):
    place = wire.place
    second = "z" if first == "x" else "x"
    own, other, core = place.at(first), place.at(second), place.core
    cut = pl.ds(low, width)
    every, low_rows, high_rows = pl.ds(0, 64), pl.ds(0, 32), pl.ds(32, 32)

    def block(spot, rows):
        if first == "x":
            return whole.at[other, core, spot, rows, cut]
        return whole.at[spot, core, other, rows, cut]

    def line(spot, part):
        if first == "x":
            return whole.at[spot, core, part, :, cut]
        return whole.at[part, core, spot, :, cut]

    def go(ref, axis, step):
        return wire.send(ref, ref, axis, step)

    right = go(block(own, every), first, 1)
    left = go(block(own, every), first, -1)
    yield gaps[0]
    right.wait_recv()
    left.wait_recv()
    right = go(block(wrap(own - 1), low_rows), first, 1)
    left = go(block(wrap(own + 1), high_rows), first, -1)
    yield gaps[1]
    right.wait_recv()
    left.wait_recv()
    right = go(line(other, FULL), second, 1)
    left = go(line(other, FULL), second, -1)
    across = [go(line(other, FULL), "core", 1)]
    yield gaps[2]
    right.wait_recv()
    left.wait_recv()
    before, after = wrap(other - 1), wrap(other + 1)
    right = go(line(before, LOW), second, 1)
    left = go(line(after, HIGH), second, -1)
    across.append(go(line(before, FULL), "core", 1))
    across.append(go(line(after, FULL), "core", 1))
    yield gaps[3]
    right.wait_recv()
    left.wait_recv()
    across.append(go(line(wrap(other + 2), FULL), "core", 1))
    yield gaps[4]
    for copy in across:
        copy.wait_recv()


def cuts(width, parts):
    return [pl.ds(part * (width // parts), width // parts) for part in range(parts)]


def ring_sum(wire, axis, mine, near, far, parts=2):
    own = wire.place.at(axis)
    before, after, facing = wrap(own - 1), wrap(own + 1), wrap(own + 2)
    half = mine.shape[1] // 2
    low_rows, high_rows = pl.ds(0, half), pl.ds(half, half)
    flights = []
    for cut in cuts(mine.shape[2], parts):
        right = wire.send(mine.at[facing, low_rows, cut], near.at[0, :, cut], axis, 1)
        left = wire.send(mine.at[facing, high_rows, cut], near.at[1, :, cut], axis, -1)
        flights.append((cut, right, left))
        yield 1
    second = []
    for cut, right, left in flights:
        right.wait_recv()
        left.wait_recv()
        mine[after, low_rows, cut] = mine[after, low_rows, cut] + near[0, :, cut]
        mine[before, high_rows, cut] = mine[before, high_rows, cut] + near[1, :, cut]
        right = wire.send(mine.at[after, :, cut], far.at[0, :, cut], axis, 1)
        left = wire.send(mine.at[before, :, cut], far.at[1, :, cut], axis, -1)
        second.append((right, left))
    yield 1
    for right, left in second:
        right.wait_recv()
        left.wait_recv()


def ring_total(wire, axis, mine, far):
    return wide(mine[wire.place.at(axis)]) + wide(far[0]) + wide(far[1])


def ring_spread(wire, axis, whole, parts=2):
    own = wire.place.at(axis)
    before, after = wrap(own - 1), wrap(own + 1)
    half = whole.shape[1] // 2
    low_rows, high_rows = pl.ds(0, half), pl.ds(half, half)

    def go(ref, step):
        return wire.send(ref, ref, axis, step)

    flights = []
    for cut in cuts(whole.shape[2], parts):
        flights.append((cut, go(whole.at[own, :, cut], 1), go(whole.at[own, :, cut], -1)))
    yield 1
    second = []
    for cut, right, left in flights:
        right.wait_recv()
        left.wait_recv()
        second.append(go(whole.at[before, low_rows, cut], 1))
        second.append(go(whole.at[after, high_rows, cut], -1))
    yield 1
    for copy in second:
        copy.wait_recv()


def owner_spot(owners, matrix, block):
    owner = owners[matrix, block]
    return lax.div(owner, 8), lax.rem(lax.div(owner, 4), 2), lax.rem(owner, 4)


def natural_rows(whole, owners, matrix, block, count, cut):
    return jnp.concatenate(
        [whole[(*owner_spot(owners, matrix, block + index), slice(None), cut)] for index in range(count)],
        axis=0,
    )


def columns(index, size):
    return pl.ds(pl.multiple_of(index * size, size), size)


def loop(count, body):
    def step(index, carry):
        body(index)
        return carry

    lax.fori_loop(0, count, step, 0)


def identity(size):
    row = lax.broadcasted_iota(jnp.int32, (size, size), 0)
    return narrow(jnp.where(row == lax.broadcasted_iota(jnp.int32, (size, size), 1), 1.0, 0.0))


def transpose_into(target, source):
    def slab(index):
        part = source[:, :, :, columns(index, 256)].reshape(256, 256)
        target[pl.ds(index * 4, 4)] = narrow(times(identity(256), part, LAST)).reshape(4, 64, 256)

    loop(8, slab)


def root_scale(value):
    return lax.rsqrt(jnp.mean(value * value, axis=-1, keepdims=True) + norm_epsilon)


def swap_halves(value):
    lane = lax.broadcasted_iota(jnp.int32, value.shape, 1)
    return jnp.where(
        lax.rem(lane, 64) < 32, pltpu.roll(value, 96, 1), pltpu.roll(value, 32, 1)
    )


def signs(shape):
    lane = lax.broadcasted_iota(jnp.int32, shape, 1)
    return jnp.where(lax.rem(lane, 64) < 32, -1.0, 1.0)


def rotate(value, cosine, sine):
    return value * cosine + swap_halves(value) * (sine * signs(value.shape))


def rotate_back(value, cosine, sine):
    return value * cosine - swap_halves(value * sine) * signs(value.shape)


EAGER = 3
FORWARD_COURSE = (
    (0, 1, 2, 3),
    (6, 7, 8),
    (0, 1, 2, 3, 5, 4),
    (6, 7),
    (1, 8, 0, 3, 2, 5, 4, 1, 0, 6, 12, 13, 14, 2, 5, 3, 4, 0, 1, 0, 1),
    (),
    (15, 16, 17),
    (9, 10, 11, 5, 13, 3, 2, 3, 2),
    (12,),
    (14,),
    (4,),
    (15,),
    (17, 9, 11, 16, 6),
    (5, 4, 7, 8, 10),
    (5, 4),
    (),
    (),
    (6, 9),
    (6, 12),
    (7,),
    (8,),
    (),
    (9,),
    (10, 7, 11),
    (),
    (),
    (7, 8, 12, 9),
    (8, 13, 9),
    (),
    (10,),
    (12, 11, 14, 12),
    (),
    (10, 13),
    (10, 15, 16),
    (11,),
    (11, 13, 14),
    (),
    (13, 17),
    (16,),
    (15, 14),
    (14,),
    (),
    (16, 17),
    (16,),
    (15,),
    (15, 17),
    (),
    (17,),
    (),
    (),
    (),
    (),
)


def forward_body(
    in_tokens,
    in_cotangent,
    segments,
    owners,
    owner_rows,
    gains,
    rates,
    m_query,
    m_key,
    m_value,
    m_output,
    m_gate,
    m_up,
    m_down,
    out_w_q,
    out_w_kv,
    out_w_out,
    out_mid,
    out_n1_t,
    out_n2,
    out_back_t,
    out_hidden,
    out_d_gate,
    out_d_up,
    out_dn,
    out_f,
    out_probs,
    out_q,
    out_kv,
    out_attended,
    out_tables,
    out_slots,
    tokens,
    cotangent,
    w_q,
    w_kv,
    w_out,
    w_gate_0,
    w_gate_1,
    w_gate_2,
    w_gate_3,
    w_up_0,
    w_up_1,
    w_up_2,
    w_up_3,
    w_down_0,
    w_down_1,
    w_down_2,
    w_down_3,
    mid_out,
    flip,
    hidden,
    d_gate,
    d_up,
    probs,
    q_out,
    kv,
    attended,
    tables,
    normed,
    normed_two,
    f_sum,
    dn_sum,
    near,
    far,
    bias,
    q_t8,
    v_t,
    o_t,
    local_sem,
    send_sem,
    recv_sem,
):
    place = Place()
    w_gate = (w_gate_0, w_gate_1, w_gate_2, w_gate_3)
    w_up = (w_up_0, w_up_1, w_up_2, w_up_3)
    w_down = (w_down_0, w_down_1, w_down_2, w_down_3)
    home = (place.z, place.core, place.x)
    local = Local(local_sem)
    staged = []
    for whole, low, master, row, column in (
        (w_kv, 0, m_key, 192, 512),
        (w_kv, 128, m_value, 192, 640),
        (w_q, 0, m_query, 192, 0),
        (w_out, 0, m_output, 192, 768),
        (w_gate, 0, m_gate, 0, 0),
        (w_up, 0, m_up, 64, 0),
        (w_down, 0, m_down, 128, 0),
    ):
        width = master.shape[1]
        spot = f_sum.at[pl.ds(row, 64), pl.ds(column, width)]
        staged.append((whole, low, width, row, spot, local.copy(master, spot)))
    load_tokens = local.copy(in_tokens, tokens)
    load_back = local.copy(in_cotangent, cotangent)
    greet(place, PARTNERS)

    def place_own(entries):
        for whole, low, width, row, spot, copy in entries:
            local.done(copy)
            if isinstance(whole, tuple):
                for part in range(4):
                    cut = pl.ds(row, 64), pl.ds(part * 512, 512)
                    whole[part][(*home, slice(None), slice(None))] = narrow(f_sum[cut])
            else:
                whole[(*home, slice(None), slice(low, low + width))] = narrow(spot[...])

    wire = Wire(place, send_sem, recv_sem)
    pump = Course(FORWARD_COURSE)
    place_own(staged[:3])
    kv_ready = [
        pump.add(gather_chunk(wire, w_kv, 0, 128, "x")),
        pump.add(gather_chunk(wire, w_kv, 128, 128, "z")),
    ]
    ready = [
        pump.add(gather_chunk(wire, w_q, 0, 256, "x")),
        pump.add(gather_chunk(wire, w_q, 256, 256, "z")),
    ]
    pump.point()
    place_own(staged[3:])
    out_ready = [
        pump.add(gather_chunk(wire, w_out, 0, 256, "x")),
        pump.add(gather_chunk(wire, w_out, 256, 256, "z")),
    ]
    down_ready, feed_ready = [], []
    for part in range(4):
        flows = [
            pump.add(gather_chunk(wire, whole[part], 0, 512, ("x", "z")[(part + number) % 2]))
            for number, whole in enumerate((w_down, w_gate, w_up))
        ]
        down_ready.append(flows[0])
        feed_ready.append(flows)

    pump.point()
    local.done(load_tokens)
    for half in range(2):
        value = wide(tokens[half]).reshape(128, WIDTH)
        normed[half] = narrow(value * root_scale(value) * gains[0:1, :]).reshape(4, 32, WIDTH)
    transpose_into(flip, normed)
    flipped = local.copy(flip, out_n1_t)
    pump.point()
    spots = lax.broadcasted_iota(jnp.int32, (7, 32), 1)
    inverse = jnp.zeros((7, 32), jnp.int32)
    for block in range(32):
        inverse = jnp.where(owner_rows[:, block : block + 1] == spots, block, inverse)
    out_slots[...] = inverse
    ids = segments[...]
    start_one = jnp.sum(jnp.where(ids < 1, 1, 0), axis=1, keepdims=True)
    start_two = jnp.sum(jnp.where(ids < 2, 1, 0), axis=1, keepdims=True)

    def begins(at):
        return jnp.where(at >= start_two, start_two, jnp.where(at >= start_one, start_one, 0))

    at = place.x * 256 + lax.broadcasted_iota(jnp.int32, (256, 128), 0)
    angle = (at - begins(at)).astype(F32) * rates[...]
    tables[0] = jnp.cos(angle)
    tables[1] = jnp.sin(angle)
    local.copy(tables, out_tables)
    pump.point()
    pump.until(kv_ready)
    local.copy(w_kv, out_w_kv)

    lhs = normed[...].reshape(256, WIDTH)
    key_rows = times(lhs, natural_rows(w_kv, owners, 1, 0, 32, slice(0, 128)))
    kv[place.x, :, 0:128] = narrow(rotate(key_rows, tables[0], tables[1]))
    value_rows = times(lhs, natural_rows(w_kv, owners, 2, 0, 32, slice(128, 256)))
    kv[place.x, :, 128:256] = narrow(value_rows)
    shares = [wire.send(kv.at[place.x], kv.at[place.x], "x", step) for step in (1, -1, 2)]

    pump.point()

    def mask(index):
        half, block = lax.div(index, 4), lax.rem(index, 4)
        at = place.x * 256 + half * 128 + lax.broadcasted_iota(jnp.int32, (1, 128), 1)
        key_at = block * 256 + lax.broadcasted_iota(jnp.int32, (256, 128), 0)
        bias[half, pl.ds(pl.multiple_of(block * 256, 256), 256), :] = jnp.where(
            (key_at <= at) & (key_at >= begins(at)), 0.0, masked_score
        )

    loop(8, mask)
    pump.point()
    local.done(load_back, flipped)
    transpose_into(flip, cotangent)
    flipped = local.copy(flip, out_back_t)

    pump.until(ready)
    local.copy(w_q, out_w_q)
    pump.point()

    def query(slab):
        cut = columns(slab, 128)
        rows = times(normed[...].reshape(256, WIDTH), natural_rows(w_q, owners, 0, 0, 32, cut))
        q_out[:, cut] = narrow(rotate(rows, tables[0], tables[1]) * SCALE)

    loop(1, query)
    pump.point()
    loop(1, lambda slab: query(slab + 1))
    pump.point()
    loop(1, lambda slab: query(slab + 2))
    pump.point()
    loop(1, lambda slab: query(slab + 3))
    local.copy(q_out, out_q)
    q_t8[...] = jnp.zeros_like(q_t8)
    for slab in range(4):
        turned = narrow(wide(q_out[:, slab * 128 : slab * 128 + 128]).T)
        goal = slice(slab // 2 * 64, slab // 2 * 64 + 64)
        for half in range(2):
            here = slice(half * 128, half * 128 + 128)
            q_t8[half * 4 + slab, goal, 0:128] = turned[0:64, here]
            q_t8[half * 4 + slab, goal, 128:256] = turned[64:128, here]
    pump.point()
    for copy in shares:
        copy.wait_recv()
    local.copy(kv, out_kv)
    for block in range(4):
        v_t[:, block * 256 : block * 256 + 256] = narrow(wide(kv[block, :, 128:256]).T)

    def attend(index, slot):
        hidden_keys = bias[lax.div(index, 4)]
        scores = times(kv[:, :, 0:128].reshape(1024, 128), q_t8[index]) + jnp.concatenate(
            [hidden_keys, hidden_keys], axis=1
        )
        top = jnp.max(scores, axis=0, keepdims=True)
        raised = jnp.exp(scores - top)
        low = narrow(raised * (1.0 / jnp.sum(raised, axis=0, keepdims=True)))
        probs[slot] = low
        goal = pl.ds(pl.multiple_of(lax.div(lax.rem(index, 4), 2) * 64, 64), 64)
        o_t[index] = times(v_t[goal, :], low)

    kept = []

    def attend_group(group):
        if group > 1:
            local.done(kept[group - 2])
        slot = group % 2 * 2
        loop(2, lambda index: attend(index + 2 * group, index + slot))
        kept.append(local.copy(probs.at[pl.ds(slot, 2)], out_probs.at[pl.ds(group * 2, 2)]))

    def project_half(half):
        here = slice(half * 128, half * 128 + 128)
        for slab in range(4):
            value = o_t[half * 4 + slab]
            both = jnp.concatenate([value[:, 0:128], value[:, 128:256]], axis=0)
            attended[here, slab * 128 : slab * 128 + 128] = narrow(both.T)

        def project(part):
            rows = natural_rows(w_out, owners, 3, part * 4, 4, slice(None))
            normed[half, :, :, columns(part, 256)] = narrow(
                times(attended[here, :], rows, LAST)
            ).reshape(4, 32, 256)

        loop(4, project)
        pump.point()
        loop(4, lambda part: project(part + 4))

    def second_norm(half):
        mid = wide(tokens[half, place.y]) + ring_total(wire, "y", normed.at[half], far.at[half])
        mid_out[half] = mid
        normed_two[half, place.y] = narrow(mid * root_scale(mid) * gains[1:2, :])

    def feed_back(part, index):
        back = cotangent[...].reshape(256, WIDTH)
        rows = natural_rows(w_down[part], owners, 6, 0, 32, columns(index, 256))
        hidden[:, columns(index + part * 2, 256)] = narrow(times(back, rows))

    def feed_back_part(part):
        pump.until(down_ready[part : part + 1])
        loop(2, lambda index: feed_back(part, index))

    sums = [ring_sum(wire, "y", normed.at[h], near.at[h], far.at[h], 1) for h in range(2)]
    spreads = [ring_spread(wire, "y", normed_two.at[h], 1) for h in range(2)]
    attend_group(0)
    pump.point()
    attend_group(1)
    pump.point()
    pump.until(out_ready)
    local.copy(w_out, out_w_out)
    project_half(0)
    next(sums[0])
    pump.point()
    attend_group(2)
    pump.point()
    next(sums[0])
    attend_group(3)
    pump.point()
    project_half(1)
    next(sums[1])
    pump.point()
    next(sums[0], None)
    second_norm(0)
    next(spreads[0])
    pump.point()
    next(sums[1])
    pump.point()
    next(spreads[0])
    local.copy(attended, out_attended)
    pump.point()
    if EAGER > 0:
        feed_back_part(0)
    pump.point()
    next(sums[1], None)
    second_norm(1)
    next(spreads[1])
    local.copy(mid_out, out_mid)
    next(spreads[0], None)
    pump.point()
    if EAGER > 1:
        feed_back_part(1)
    next(spreads[1])
    pump.point()
    if EAGER > 2:
        feed_back_part(2)
    next(spreads[1], None)

    def feed(part, index):
        cut = columns(index + part * 2, 256)
        here = columns(index, 256)
        lhs = normed_two[...].reshape(256, WIDTH)
        gate = times(lhs, natural_rows(w_gate[part], owners, 4, 0, 32, here))
        up = times(lhs, natural_rows(w_up[part], owners, 5, 0, 32, here))
        d_hidden = wide(hidden[:, cut])
        sigmoid = jax.nn.sigmoid(gate)
        silu = gate * sigmoid
        hidden[:, cut] = narrow(silu * up)
        d_gate[:, cut] = narrow(d_hidden * up * sigmoid * (1.0 + gate * (1.0 - sigmoid)))
        d_up[:, cut] = narrow(d_hidden * silu)

    def project_feed(part):
        units = slice(part * 512, part * 512 + 512)

        def rows_of(whole, matrix, index):
            return natural_rows(whole[part], owners, matrix, index * 4, 4, slice(None))

        def tile(index):
            cut = columns(index, 256)
            down = times(hidden[:, units], rows_of(w_down, 6, index), LAST)
            back = times(
                jnp.concatenate([d_gate[:, units], d_up[:, units]], axis=1),
                jnp.concatenate([rows_of(w_gate, 4, index), rows_of(w_up, 5, index)], axis=1),
                LAST,
            )
            if part > 0:
                down = f_sum[:, cut] + down
                back = dn_sum[:, cut] + back
            if part < 3:
                f_sum[:, cut] = down
                dn_sum[:, cut] = back
            else:
                normed_two[:, :, :, cut] = narrow(down).reshape(2, 4, 32, 256)
                normed[:, :, :, cut] = narrow(back).reshape(2, 4, 32, 256)

        loop(4, tile)
        pump.point()
        loop(4, lambda index: tile(index + 4))

    for part in range(4):
        if part >= EAGER:
            feed_back_part(part)
        pump.until(feed_ready[part])
        loop(1, lambda index: feed(part, index))
        pump.point()
        loop(1, lambda index: feed(part, index + 1))
        pump.point()
        if part == 0:
            local.copy(normed_two, out_n2)
        if part == 3:
            wire.finish()
            local.finish()
            for source, target in ((hidden, out_hidden), (d_gate, out_d_gate), (d_up, out_d_up)):
                local.copy(source, target)
        project_feed(part)
        pump.point()
    local.copy(normed, out_dn)
    local.copy(normed_two, out_f)
    local.finish()


def forward(tokens, cotangent, segments, owners, gains, masters):
    def shape(*sizes, dtype=BF16):
        return jax.ShapeDtypeStruct(sizes, dtype)

    rates = jnp.asarray(np.tile(rope_frequencies(HEAD_SIZE), 4)[None, :])
    outs = [
        shape(4, 2, 4, 64, 512),
        shape(4, 2, 4, 64, 256),
        shape(4, 2, 4, 64, 512),
        shape(2, 32, WIDTH, dtype=F32),
        shape(32, 64, 256),
        shape(2, 4, 32, WIDTH),
        shape(32, 64, 256),
        shape(256, WIDTH),
        shape(256, WIDTH),
        shape(256, WIDTH),
        shape(2, 4, 32, WIDTH),
        shape(2, 4, 32, WIDTH),
        shape(8, 1024, 256),
        shape(256, 512),
        shape(4, 256, 256),
        shape(256, 512),
        shape(2, 256, 128, dtype=F32),
        shape(7, 32, dtype=jnp.int32),
    ]
    scratch = [
        pltpu.VMEM((2, 4, 32, WIDTH), BF16),
        pltpu.VMEM((2, 4, 32, WIDTH), BF16),
        pltpu.VMEM((4, 2, 4, 64, 512), BF16),
        pltpu.VMEM((4, 2, 4, 64, 256), BF16),
        pltpu.VMEM((4, 2, 4, 64, 512), BF16),
        *[pltpu.VMEM((4, 2, 4, 64, 512), BF16)] * 12,
        pltpu.VMEM((2, 32, WIDTH), F32),
        pltpu.VMEM((32, 64, 256), BF16),
        pltpu.VMEM((256, WIDTH), BF16),
        pltpu.VMEM((256, WIDTH), BF16),
        pltpu.VMEM((256, WIDTH), BF16),
        pltpu.VMEM((4, 1024, 256), BF16),
        pltpu.VMEM((256, 512), BF16),
        pltpu.VMEM((4, 256, 256), BF16),
        pltpu.VMEM((256, 512), BF16),
        pltpu.VMEM((2, 256, 128), F32),
        pltpu.VMEM((2, 4, 32, WIDTH), BF16),
        pltpu.VMEM((2, 4, 32, WIDTH), BF16),
        pltpu.VMEM((256, WIDTH), F32),
        pltpu.VMEM((256, WIDTH), F32),
        pltpu.VMEM((2, 2, 16, WIDTH), BF16),
        pltpu.VMEM((2, 2, 32, WIDTH), BF16),
        pltpu.VMEM((2, 1024, 128), F32),
        pltpu.VMEM((8, 128, 256), BF16),
        pltpu.VMEM((128, 1024), BF16),
        pltpu.VMEM((8, 64, 256), F32),
        pltpu.SemaphoreType.DMA((40,)),
        pltpu.SemaphoreType.DMA((240,)),
        pltpu.SemaphoreType.DMA((240,)),
    ]
    return pl.pallas_call(
        forward_body,
        out_shape=outs,
        in_specs=[ANYWHERE] * 2 + [IN_VMEM, IN_SMEM] + [IN_VMEM] * 3 + [ANYWHERE] * 7,
        out_specs=[ANYWHERE] * (len(outs) - 1) + [IN_VMEM],
        scratch_shapes=scratch,
        compiler_params=pltpu.CompilerParams(
            collective_id=1, has_side_effects=True, vmem_limit_bytes=VMEM_BYTES
        ),
        name="forward",
    )(
        tokens.reshape(2, 4, 32, WIDTH),
        cotangent.reshape(2, 4, 32, WIDTH),
        segments,
        owners,
        owners,
        gains,
        rates,
        *masters,
    )


DEPTH = 8
SIDES = (("x", 1), ("x", -1), ("z", 1), ("z", -1), ("core", 1))


def reduce_chunk(wire, fill, slot, buffers, credit, take, give, first, finish, gap):
    place = wire.place
    second = "z" if first == "x" else "x"
    own, other, core = place.at(first), place.at(second), place.core
    pieces, near, far, one, two = buffers
    if take:
        for side in range(5):
            pl.semaphore_wait(credit.at[side], 1)
    fill(slot)
    copies = [wire.send(slot.at[:, 1 - core], pieces, "core", 1)]
    yield 1
    copies[0].wait_recv()

    def add_pair(row):
        pieces[row] = pieces[row] + slot[row, core]

    loop(4, add_pair)
    wire.sent(copies[:1])

    def spot(line, place_in):
        return (line, place_in) if first == "z" else (place_in, line)

    before, after, facing = wrap(own - 1), wrap(own + 1), wrap(own + 2)
    right = wire.send(pieces.at[spot(facing, LOW)], near.at[0], first, 1)
    left = wire.send(pieces.at[spot(facing, HIGH)], near.at[1], first, -1)
    copies += [right, left]
    yield gap
    right.wait_recv()
    left.wait_recv()
    here = spot(after, LOW)
    pieces[here] = pieces[here] + near[0]
    here = spot(before, HIGH)
    pieces[here] = pieces[here] + near[1]
    right = wire.send(pieces.at[spot(after, FULL)], far.at[0], first, 1)
    left = wire.send(pieces.at[spot(before, FULL)], far.at[1], first, -1)
    copies += [right, left]
    yield gap
    right.wait_recv()
    left.wait_recv()
    here = spot(own, FULL)
    pieces[here] = narrow(wide(pieces[here]) + wide(far[0]) + wide(far[1]))
    before, after, facing = wrap(other - 1), wrap(other + 1), wrap(other + 2)
    low_rows, high_rows = pl.ds(0, 32), pl.ds(32, 32)
    right = wire.send(pieces.at[spot(own, facing) + (low_rows,)], one.at[0], second, 1)
    left = wire.send(pieces.at[spot(own, facing) + (high_rows,)], one.at[1], second, -1)
    copies += [right, left]
    yield 1
    right.wait_recv()
    left.wait_recv()
    here = spot(own, after) + (low_rows,)
    pieces[here] = pieces[here] + one[0]
    here = spot(own, before) + (high_rows,)
    pieces[here] = pieces[here] + one[1]
    right = wire.send(pieces.at[spot(own, after)], two.at[0], second, 1)
    left = wire.send(pieces.at[spot(own, before)], two.at[1], second, -1)
    copies += [right, left]
    yield 1
    right.wait_recv()
    left.wait_recv()
    finish(wide(pieces[spot(own, other)]) + wide(two[0]) + wide(two[1]))
    wire.sent(copies[1:])
    if give:
        for side, (axis, step) in enumerate(SIDES):
            back = SIDES.index((axis, -step)) if axis != "core" else 4
            pl.semaphore_signal(
                credit.at[back], inc=1, device_id=place.toward(axis, step), device_id_type=MESH
            )


SLOTS = 2
TURNS = 15
FEED_FIRST, FEED_SECOND = 9, 12
BACKWARD_COURSE = (
    (),
    (0, 1),
    (),
    (0, 2, 1, 3),
    (2, 0, 4, 3),
    (1, 5, 2, 4),
    (6, 3, 5),
    (),
    (0, 6),
    (1, 2),
    (4,),
    (0, 2, 3, 5, 6),
    (0, 1, 4),
    (3, 6, 1, 2, 7, 4, 5, 8),
    (3, 7, 4, 6, 5, 12, 8, 9),
    (),
    (7, 12),
    (5, 6, 9, 8, 10, 11, 12),
    (),
    (7, 10, 11),
    (8, 9, 13, 14),
    (8, 12, 7, 13, 14),
    (11, 10, 7, 15, 9),
    (8, 13, 15, 16),
    (16,),
    (12,),
    (14, 17, 11, 9, 17, 10, 16, 13, 15, 12, 9, 17, 10, 14, 11, 15, 16, 17, 13, 10, 11, 14, 15, 16, 17, 13, 15, 14, 17, 16),
)


def backward_body(
    in_tokens,
    in_cotangent,
    owners,
    slots,
    gains,
    in_w_q,
    in_w_kv,
    in_w_out,
    in_mid,
    in_n1_t,
    in_n2,
    in_back_t,
    in_hidden,
    in_d_gate,
    in_d_up,
    dn_in,
    f_in,
    in_probs,
    in_queries,
    in_kv,
    in_attended,
    in_tables,
    out_output,
    out_grad_low,
    out_query,
    out_key,
    out_value,
    out_output_grad,
    out_gate,
    out_up,
    out_down,
    g_gains,
    tokens,
    cotangent,
    output,
    grad_low,
    g_query,
    g_key,
    g_value,
    g_output,
    g_gate,
    g_up,
    g_down,
    w_qkv,
    w_out,
    mid,
    n1_t,
    n2_t,
    back_t,
    hidden,
    d_gate,
    d_up,
    probs,
    queries,
    kv,
    attended,
    tables,
    pieces,
    near,
    far,
    one,
    two,
    fills,
    gain_fill,
    dn_mine,
    dn_near,
    dn_far,
    f_mine,
    f_near,
    f_far,
    n_mine,
    n_near,
    n_far,
    kv_mine,
    kv_near,
    kv_far,
    da,
    da_t,
    d_mid,
    d_t8,
    d_8,
    q_8,
    k_t,
    dq_t,
    dk_sum,
    dv_sum,
    d_query,
    d_key,
    d_value,
    gain_rows,
    gain_all,
    scales,
    credit,
    local_sem,
    send_sem,
    recv_sem,
):
    place = Place()
    local = Local(local_sem)
    load_dn = local.copy(dn_in, dn_mine)
    load_down = [local.copy(in_back_t, back_t), local.copy(in_hidden, hidden)]
    load_n2 = local.copy(in_n2, da)
    load_gate = [local.copy(in_d_gate, d_gate)]
    load_up = [local.copy(in_d_up, d_up)]
    load_mid = [
        local.copy(in_cotangent, cotangent),
        local.copy(in_mid, mid),
        local.copy(in_w_out, w_out),
    ]
    load_heads = [
        local.copy(in_kv, kv),
        local.copy(in_queries, queries),
        local.copy(in_probs.at[pl.ds(0, 2)], probs.at[pl.ds(0, 2)]),
        local.copy(in_probs.at[pl.ds(2, 2)], probs.at[pl.ds(2, 2)]),
    ]
    load_f = local.copy(f_in, f_mine)
    load_out = [local.copy(in_attended, attended)]
    load_late = [
        local.copy(in_tokens, tokens),
        local.copy(in_tables, tables),
        local.copy(in_w_q, w_qkv.at[:, :, :, :, pl.ds(0, 512)]),
        local.copy(in_w_kv, w_qkv.at[:, :, :, :, pl.ds(512, 256)]),
        local.copy(in_n1_t, n1_t),
    ]
    greet(place, PARTNERS)
    wire = Wire(place, send_sem, recv_sem)
    pump = Course(BACKWARD_COURSE)
    def chunk_flow(turn, slot, low, width, fill, finish, take, give, first, gap):
        size = pl.ds(low, width)
        buffers = [
            pieces.at[turn, :, :, :, size],
            near.at[turn, :, :, :, size],
            far.at[turn, :, :, :, size],
            one.at[turn, :, :, size],
            two.at[turn, :, :, size],
        ]
        space = gain_fill if slot is None else fills.at[slot, :, :, :, :, size]
        return reduce_chunk(wire, fill, space, buffers, credit, take, give, first, finish, gap)

    def product(matrix, left, right, low, width, loads=()):
        def fill(slot):
            local.done(*loads)

            def rows(index):
                lhs = jnp.concatenate(
                    [left[slots[matrix, index * 16 + step]] for step in range(16)], axis=0
                )
                slot[pl.ds(index * 2, 2)] = narrow(
                    times(lhs, right[:, pl.ds(low, width)])
                ).reshape(2, 2, 4, 64, width)

            loop(2, rows)

        return fill

    def keep(target, out, low, width):
        def finish(value):
            cut = pl.ds(low, width)
            target[:, cut] = value
            local.copy(target.at[:, cut], out.at[:, cut])

        return finish

    def add_feed(turn, matrix, left, right, target, out, low, loads=()):
        flow = chunk_flow(
            turn % DEPTH,
            turn % SLOTS,
            0,
            512,
            product(matrix, left, right, low, 512, loads),
            keep(target, out, low, 512),
            turn >= DEPTH,
            turn < TURNS - DEPTH,
            ("x", "z")[turn // 2 % 2],
            1,
        )
        pump.add(flow, turn)

    def add_rest(turn, parts):
        for matrix, right, target, out, low, width, at, first in parts:
            flow = chunk_flow(
                turn % DEPTH,
                turn % SLOTS,
                at,
                width,
                product(matrix, n1_t, right, low, width),
                keep(target, out, low, width),
                at == 0,
                turn < TURNS - DEPTH,
                first,
                1,
            )
            pump.add(flow, turn)

    turn_of = {}
    for number in range(12):
        turn_of[number] = number + (number >= FEED_FIRST) + (number >= FEED_SECOND)
    out_turn, query_turn = FEED_FIRST, FEED_SECOND + 1
    for part in range(4):
        loads = () if part else load_down
        add_feed(turn_of[part], 6, back_t, hidden, g_down, out_down, part * 512, loads)
    local.done(load_dn)
    def halves(mine, near_rows, far_rows, parts):
        return [
            ring_sum(wire, "y", mine.at[h], near_rows.at[h], far_rows.at[h], parts)
            for h in range(2)
        ]

    def norm_back(half):
        mine = mid[half]
        scale = root_scale(mine)
        hat = mine * scale
        total = ring_total(wire, "y", dn_mine.at[half], dn_far.at[half])
        gained = jnp.sum(total * hat, axis=0, keepdims=True)
        gain_rows[1:2, :] = gained if half == 0 else gain_rows[1:2, :] + gained
        scaled = total * gains[1:2, :]
        value = wide(cotangent[half, place.y]) + scale * (
            scaled - hat * jnp.mean(scaled * hat, axis=-1, keepdims=True)
        )
        d_mid[half] = value
        da[half, place.y] = narrow(value)

    lane = lax.broadcasted_iota(jnp.int32, (128, 128), 1)

    def heads_of(half):
        here = slice(half * 128, half * 128 + 128)

        def attended_back(slab):
            cut = columns(slab, 256)
            rows = times(
                da[half].reshape(128, WIDTH), natural_rows(w_out, owners, 3, 0, 32, cut)
            )
            d_query[here, cut] = narrow(rows)

        loop(2, attended_back)
        for slab in range(4):
            goal = slab // 2
            cut = slice(slab * 128, slab * 128 + 128)
            index = half * 4 + slab
            for source, rows in ((queries, q_8), (d_query, d_8)):
                value = wide(source[here, cut])
                for side in range(2):
                    moved = value if side == goal else pltpu.roll(value, 64, 1)
                    rows[index, side * 128 : side * 128 + 128, :] = narrow(
                        jnp.where((lane < 64) == (goal == 0), moved, 0.0)
                    )
            turned = narrow(wide(d_query[here, cut]).T)
            d_t8[index, goal * 64 : goal * 64 + 64, 0:128] = turned[0:64]
            d_t8[index, goal * 64 : goal * 64 + 64, 128:256] = turned[64:128]

    sums = halves(dn_mine, dn_near, dn_far, 1)
    spreads = [ring_spread(wire, "y", da.at[h], 1) for h in range(2)]
    next(sums[0])
    next(sums[1])
    pump.point()
    local.done(load_n2)
    transpose_into(n2_t, da)
    for part in range(4):
        cut = part * 512
        loads = () if part else load_gate
        add_feed(turn_of[4 + 2 * part], 4, n2_t, d_gate, g_gate, out_gate, cut, loads)
        loads = () if part else load_up
        add_feed(turn_of[5 + 2 * part], 5, n2_t, d_up, g_up, out_up, cut, loads)
    pump.point()
    next(sums[0])
    pump.point()
    next(sums[1])
    local.done(*load_mid)
    d_t8[...] = jnp.zeros_like(d_t8)
    dk_sum[...] = jnp.zeros_like(dk_sum)
    dv_sum[...] = jnp.zeros_like(dv_sum)
    pump.point()
    next(sums[0], None)
    norm_back(0)
    next(spreads[0])
    pump.point()
    next(sums[1], None)
    norm_back(1)
    next(spreads[1])
    local.done(*load_heads[:2])
    for block in range(4):
        k_t[:, block * 256 : block * 256 + 256] = narrow(wide(kv[block, :, 0:128]).T)
    pump.point()
    next(spreads[0])
    pump.point()
    next(spreads[1])
    pump.point()
    next(spreads[0], None)
    heads_of(0)
    pump.point()

    def attend_back(index, slot):
        low = probs[slot]
        prob = wide(low)
        d_prob = times(kv[:, :, 128:256].reshape(1024, 128), d_t8[index])
        kept = prob * d_prob
        d_score = narrow(kept - prob * jnp.sum(kept, axis=0, keepdims=True))
        goal = pl.ds(pl.multiple_of(lax.div(lax.rem(index, 4), 2) * 64, 64), 64)
        dq_t[index] = times(k_t[goal, :], d_score)
        dv_sum[...] += times(low, d_8[index])
        dk_sum[...] += times(d_score, q_8[index])

    coming = load_heads[2:]

    def attend_group(group):
        slot = group % 2 * 2
        local.done(coming[group % 2])
        loop(2, lambda index: attend_back(index + 2 * group, index + slot))
        if group < 2:
            here = pl.ds(slot, 2)
            coming[group % 2] = local.copy(in_probs.at[pl.ds(group * 2 + 4, 2)], probs.at[here])

    attend_group(0)
    pump.point()
    attend_group(1)
    pump.point()
    next(spreads[1], None)
    heads_of(1)
    local.done(load_f)
    f_flows = halves(f_mine, f_near, f_far, 1)
    for flow in f_flows:
        next(flow)
    transpose_into(da_t, da)
    add_feed(out_turn, 3, da_t, attended, g_output, out_output_grad, 0, load_out)
    pump.point()
    attend_group(2)
    for flow in f_flows:
        next(flow)
    pump.point()
    attend_group(3)
    kv_mine[:, :, 0:128] = narrow(dk_sum[...]).reshape(4, 256, 128)
    kv_mine[:, :, 128:256] = narrow(dv_sum[...]).reshape(4, 256, 128)
    kv_flow = ring_sum(wire, "x", kv_mine, kv_near, kv_far, 1)
    next(kv_flow)
    local.done(*load_late)
    for slab in range(4):
        cut = slice(slab * 128, slab * 128 + 128)
        for half in range(2):
            here = slice(half * 128, half * 128 + 128)
            value = dq_t[half * 4 + slab]
            both = jnp.concatenate([value[:, 0:128], value[:, 128:256]], axis=0).T * SCALE
            d_query[here, cut] = narrow(rotate_back(both, tables[0, here], tables[1, here]))
    add_rest(
        query_turn,
        (
            (0, d_query, g_query, out_query, 0, 256, 0, "x"),
            (0, d_query, g_query, out_query, 256, 256, 256, "z"),
        ),
    )
    pump.point()
    next(kv_flow)
    for half in range(2):
        next(f_flows[half], None)
        output[half, place.y] = narrow(
            mid[half] + ring_total(wire, "y", f_mine.at[half], f_far.at[half])
        )
    out_flows = [ring_spread(wire, "y", output.at[h], 1) for h in range(2)]
    for flow in out_flows:
        next(flow)
    for half in range(2):
        value = wide(tokens[half]).reshape(128, WIDTH)
        scales[half] = jnp.broadcast_to(root_scale(value), (128, 128))
    pump.point()
    for _ in kv_flow:
        pass
    total = ring_total(wire, "x", kv_mine, kv_far)
    d_key[...] = narrow(rotate_back(total[:, 0:128], tables[0], tables[1]))
    d_value[...] = narrow(total[:, 128:256])
    add_rest(
        TURNS - 1,
        (
            (1, d_key, g_key, out_key, 0, 128, 0, "x"),
            (2, d_value, g_value, out_value, 0, 128, 128, "z"),
        ),
    )
    pump.point()

    def project_back(index):
        cut = columns(index, 256)
        first = index * 4
        rows = [
            natural_rows(w_qkv, owners, matrix, first, 4, here)
            for matrix, here in enumerate((slice(0, 512), slice(512, 640), slice(640, 768)))
        ]
        part = times(
            jnp.concatenate([d_query[...], d_key[...], d_value[...]], axis=1),
            jnp.concatenate(rows, axis=1),
            LAST,
        )
        n_mine[:, :, :, cut] = narrow(part).reshape(2, 4, 32, 256)
        hat = wide(tokens[:, :, :, cut]).reshape(256, 256) * scales[:, :, 0:1].reshape(256, 1)
        gain_rows[0:1, cut] = jnp.sum(part * hat, axis=0, keepdims=True)

    n_flows = halves(n_mine, n_near, n_far, 2)
    loop(2, project_back)
    pump.point()
    loop(2, lambda index: project_back(index + 2))
    for flow in n_flows:
        next(flow)
    pump.point()
    loop(2, lambda index: project_back(index + 4))
    pump.point()
    loop(2, lambda index: project_back(index + 6))
    for flow in n_flows:
        next(flow)
    for flow in out_flows:
        next(flow)

    def gain_chunk(slot):
        slot[...] = jnp.zeros_like(slot)
        for block in range(32):
            low = block // 2 * 128
            slot[block // 8, block // 4 % 2, block % 4, 0:2, :] = narrow(
                gain_rows[0:2, low : low + 128]
            )

    def gain_finish(value):
        gain_all[place.y] = value[0:8]

    gain_flow = chunk_flow(
        (TURNS - 1) % DEPTH, None, 256, 128, gain_chunk, gain_finish, False, False, "x", 1
    )
    pump.add(gain_flow, TURNS)
    pump.point()
    for flow in n_flows:
        next(flow)
    for flow in out_flows:
        next(flow, None)
    local.copy(output, out_output)
    spreads = [ring_spread(wire, "y", grad_low.at[h], 1) for h in range(2)]
    for half in range(2):
        pump.point()
        next(n_flows[half], None)
        value = wide(tokens[half, place.y])
        scale = root_scale(value)
        hat = value * scale
        total = ring_total(wire, "y", n_mine.at[half], n_far.at[half])
        scaled = total * gains[0:1, :]
        grad_low[half, place.y] = narrow(
            d_mid[half]
            + scale * (scaled - hat * jnp.mean(scaled * hat, axis=-1, keepdims=True))
        )
        next(spreads[half])
    for flow in spreads:
        pump.point()
        next(flow)
    for flow in spreads:
        pump.point()
        next(flow, None)
    local.copy(grad_low, out_grad_low)
    pump.until(tuple(range(len(pump.flows))))
    shares = [
        wire.send(gain_all.at[place.y], gain_all.at[place.y], "y", step) for step in (1, -1, 2)
    ]
    for copy in shares:
        copy.wait_recv()
    g_gains[...] = gain_all[0] + gain_all[1] + gain_all[2] + gain_all[3]
    wire.finish()
    local.finish()


def backward(tokens, cotangent, owners, gains, kept):
    def shape(*sizes, dtype=BF16):
        return jax.ShapeDtypeStruct(sizes, dtype)

    *kept, slots = kept
    outs = [
        shape(2, 4, 32, WIDTH),
        shape(2, 4, 32, WIDTH),
        shape(64, 512, dtype=F32),
        shape(64, 128, dtype=F32),
        shape(64, 128, dtype=F32),
        shape(64, 512, dtype=F32),
        shape(64, 2048, dtype=F32),
        shape(64, 2048, dtype=F32),
        shape(64, 2048, dtype=F32),
        shape(8, 128, dtype=F32),
    ]
    scratch = [
        *[pltpu.VMEM((2, 4, 32, WIDTH), BF16)] * 4,
        *[pltpu.VMEM(out.shape, F32) for out in outs[2:9]],
        pltpu.VMEM((4, 2, 4, 64, 768), BF16),
        pltpu.VMEM((4, 2, 4, 64, 512), BF16),
        pltpu.VMEM((2, 32, WIDTH), F32),
        pltpu.VMEM((32, 64, 256), BF16),
        pltpu.VMEM((32, 64, 256), BF16),
        pltpu.VMEM((32, 64, 256), BF16),
        pltpu.VMEM((256, WIDTH), BF16),
        pltpu.VMEM((256, WIDTH), BF16),
        pltpu.VMEM((256, WIDTH), BF16),
        pltpu.VMEM((4, 1024, 256), BF16),
        pltpu.VMEM((256, 512), BF16),
        pltpu.VMEM((4, 256, 256), BF16),
        pltpu.VMEM((256, 512), BF16),
        pltpu.VMEM((2, 256, 128), F32),
        pltpu.VMEM((DEPTH, 4, 4, 64, 512), BF16),
        pltpu.VMEM((DEPTH, 2, 2, 64, 512), BF16),
        pltpu.VMEM((DEPTH, 2, 4, 64, 512), BF16),
        pltpu.VMEM((DEPTH, 2, 32, 512), BF16),
        pltpu.VMEM((DEPTH, 2, 64, 512), BF16),
        pltpu.VMEM((SLOTS, 4, 2, 4, 64, 512), BF16),
        pltpu.VMEM((4, 2, 4, 64, 128), BF16),
        *[
            pltpu.VMEM(sizes, BF16)
            for sizes in ((2, 4, 32, WIDTH), (2, 2, 16, WIDTH), (2, 2, 32, WIDTH)) * 3
        ],
        pltpu.VMEM((4, 256, 256), BF16),
        pltpu.VMEM((2, 128, 256), BF16),
        pltpu.VMEM((2, 256, 256), BF16),
        pltpu.VMEM((2, 4, 32, WIDTH), BF16),
        pltpu.VMEM((32, 64, 256), BF16),
        pltpu.VMEM((2, 32, WIDTH), F32),
        pltpu.VMEM((8, 128, 256), BF16),
        pltpu.VMEM((8, 256, 128), BF16),
        pltpu.VMEM((8, 256, 128), BF16),
        pltpu.VMEM((128, 1024), BF16),
        pltpu.VMEM((8, 64, 256), F32),
        pltpu.VMEM((1024, 128), F32),
        pltpu.VMEM((1024, 128), F32),
        pltpu.VMEM((256, 512), BF16),
        pltpu.VMEM((256, 128), BF16),
        pltpu.VMEM((256, 128), BF16),
        pltpu.VMEM((8, WIDTH), F32),
        pltpu.VMEM((4, 8, 128), F32),
        pltpu.VMEM((2, 128, 128), F32),
        pltpu.SemaphoreType.REGULAR((5,)),
        pltpu.SemaphoreType.DMA((64,)),
        pltpu.SemaphoreType.DMA((240,)),
        pltpu.SemaphoreType.DMA((240,)),
    ]
    specs = [ANYWHERE, ANYWHERE, IN_SMEM, IN_SMEM, IN_VMEM] + [ANYWHERE] * len(kept)
    return pl.pallas_call(
        backward_body,
        out_shape=outs,
        in_specs=specs,
        out_specs=[ANYWHERE] * 9 + [IN_VMEM],
        scratch_shapes=scratch,
        compiler_params=pltpu.CompilerParams(
            collective_id=2, has_side_effects=True, vmem_limit_bytes=VMEM_BYTES
        ),
        name="backward",
    )(
        tokens.reshape(2, 4, 32, WIDTH),
        cotangent.reshape(2, 4, 32, WIDTH),
        owners,
        slots,
        gains,
        *kept,
    )


def split_dot(left, right, contract=((1,), (0,))):
    high_left, high_right = narrow(left), narrow(right)
    low_left = narrow(left - wide(high_left))
    low_right = narrow(right - wide(high_right))
    return (
        times(high_left, high_right, contract)
        + times(high_left, low_right, contract)
        + times(low_left, high_right, contract)
    )


def update_body(count, *refs):
    in_output, in_grad, gains, gain_moments, gain_grad = refs[:5]
    ins, refs = refs[5 : 5 + 3 * count], refs[5 + 3 * count :]
    out_output, out_grad, new_gains, new_gain_moments = refs[:4]
    outs, refs = refs[4 : 4 + 2 * count], refs[4 + 2 * count :]
    output, grad_low, grad_wide, copy_sem = refs[0], refs[1], refs[2], refs[-1]
    space, directions = refs[3 : 3 + 3 * count], refs[3 + 3 * count : 3 + 4 * count]
    masters, moments, grads = space[:count], space[count : 2 * count], space[2 * count :]
    local = Local(copy_sem)
    order = sorted(range(count), key=lambda number: -ins[number].shape[1])
    loads = {}
    for number in order:
        loads[number] = [
            local.copy(ins[2 * count + number], grads[number]),
            local.copy(ins[count + number], moments[number]),
        ]
    load_grad = local.copy(in_grad, grad_low)
    load_output = local.copy(in_output, output)
    load_masters = [local.copy(ins[number], masters[number]) for number in range(count)]
    first, second, third = newton_coeffs
    grams = [None] * count
    for number in order:
        local.done(*loads[number])
        grad = grads[number][...]
        renewed = momentum_decay * moments[number][...] + grad
        moments[number][...] = renewed
        local.copy(moments[number], outs[count + number])
        direction = grad + momentum_decay * renewed
        direction = direction * (1.0 / (jnp.sqrt(jnp.sum(direction * direction)) + 1e-07))
        directions[number][...] = direction
        grams[number] = split_dot(direction, direction, LAST)
    local.done(load_output, load_grad)
    local.copy(output, out_output)
    for half in range(2):
        grad_wide[half * 128 : half * 128 + 128, :] = wide(grad_low[half]).reshape(128, WIDTH)
    local.copy(grad_wide, out_grad)
    spot = lax.axis_index("dp") * 4 + lax.axis_index("ctx")
    odd = lax.rem(spot, 2) == 1

    def half(value):
        return jnp.where(odd, pltpu.roll(value, 64, 1), value)[:, 0:64]

    grad = half(gain_grad[...])[0:2]
    slab = gains[:, columns(lax.div(spot, 2), 128)]
    renewed = momentum_decay * gain_moments[...] + grad
    new_gain_moments[...] = renewed
    new_gains[...] = half(jnp.concatenate([slab] * 4, axis=0))[0:2] - gain_rate * (
        grad + momentum_decay * renewed
    )
    factors = [None] * count
    diagonal = lax.broadcasted_iota(jnp.int32, (64, 64), 0) == lax.broadcasted_iota(
        jnp.int32, (64, 64), 1
    )
    for sweep in range(5):
        squares = [split_dot(gram, gram) for gram in grams]
        steps = [
            jnp.where(diagonal, first, 0.0) + second * gram + third * square
            for gram, square in zip(grams, squares)
        ]
        if sweep == 0:
            factors = steps
            part = [split_dot(step, gram) for step, gram in zip(steps, grams)]
        elif sweep < 4:
            both = [
                split_dot(step, jnp.concatenate([gram, factor], axis=1))
                for step, gram, factor in zip(steps, grams, factors)
            ]
            part = [value[:, 0:64] for value in both]
            factors = [value[:, 64:128] for value in both]
        else:
            factors = [split_dot(step, factor) for step, factor in zip(steps, factors)]
        if sweep < 4:
            grams = [split_dot(piece, step) for piece, step in zip(part, steps)]
    local.done(*load_masters)
    for number in order:
        scale = learning_rate * 0.2 * math.sqrt(max(64, masters[number].shape[1]))
        update = split_dot(factors[number], directions[number][...])
        masters[number][...] = (
            masters[number][...] * (1.0 - learning_rate * weight_decay) - scale * update
        )
        local.copy(masters[number], outs[number])
    local.finish()


def update_blocks(output, grad_low, gains, gain_moments, gain_grad, masters, moments, grads):
    count = len(masters)
    shapes = [jax.ShapeDtypeStruct(master.shape, F32) for master in masters]
    results = pl.pallas_call(
        lambda *refs: update_body(count, *refs),
        out_shape=[
            jax.ShapeDtypeStruct((256, WIDTH), BF16),
            jax.ShapeDtypeStruct((256, WIDTH), F32),
            jax.ShapeDtypeStruct(gain_moments.shape, F32),
            jax.ShapeDtypeStruct(gain_moments.shape, F32),
        ]
        + shapes
        + shapes,
        in_specs=[ANYWHERE] * 2 + [IN_VMEM] * 3 + [ANYWHERE] * (3 * count),
        out_specs=[ANYWHERE] * 2 + [IN_VMEM] * 2 + [ANYWHERE] * (2 * count),
        scratch_shapes=[
            pltpu.VMEM((256, WIDTH), BF16),
            pltpu.VMEM((2, 4, 32, WIDTH), BF16),
            pltpu.VMEM((256, WIDTH), F32),
        ]
        + [pltpu.VMEM(master.shape, F32) for master in masters] * 4
        + [pltpu.SemaphoreType.DMA((5 * count + 4,))],
        compiler_params=pltpu.CompilerParams(vmem_limit_bytes=VMEM_BYTES),
        name="update_blocks",
    )(
        output.reshape(256, WIDTH),
        grad_low,
        gains,
        gain_moments,
        gain_grad,
        *masters,
        *moments,
        *grads,
    )
    return results[:4], results[4 : 4 + count], results[4 + count :]


def on_device(
    tokens,
    cotangent,
    segments,
    owners,
    gains,
    gain_moments,
    query_master,
    key_master_blocks,
    value_master_blocks,
    output_master,
    gate_master,
    up_master,
    down_master,
    query_moment,
    key_momentum,
    value_momentum,
    output_moment,
    gate_moment,
    up_moment,
    down_moment,
):
    masters = (
        query_master,
        key_master_blocks,
        value_master_blocks,
        output_master,
        gate_master,
        up_master,
        down_master,
    )
    moments = (
        query_moment,
        key_momentum,
        value_momentum,
        output_moment,
        gate_moment,
        up_moment,
        down_moment,
    )
    kept = forward(tokens, cotangent, segments, owners, gains, masters)
    output, grad_low, *grads, gain_grad = backward(tokens, cotangent, owners, gains, kept)
    firsts, new_masters, new_moments = update_blocks(
        output, grad_low, gains, gain_moments, gain_grad, masters, moments, grads
    )
    return tuple(firsts[:2]) + tuple(new_masters) + tuple(new_moments) + tuple(firsts[2:])


def solution(mesh):
    return jax.shard_map(
        on_device,
        mesh=mesh,
        in_specs=(
            P(("dp", "ctx"), None),
            P(("dp", "ctx"), None),
            P("dp", None),
            P(),
            P(),
            P(None, ("dp", "ctx")),
            P(("dp", "ctx"), "tensor"),
            P(("dp", "ctx"), "tensor"),
            P(("dp", "ctx"), "tensor"),
            P(("dp", "ctx"), "tensor"),
            P(("dp", "ctx"), "tensor"),
            P(("dp", "ctx"), "tensor"),
            P(("dp", "ctx"), "tensor"),
            P(("dp", "ctx"), "tensor"),
            P(("dp", "ctx"), "tensor"),
            P(("dp", "ctx"), "tensor"),
            P(("dp", "ctx"), "tensor"),
            P(("dp", "ctx"), "tensor"),
            P(("dp", "ctx"), "tensor"),
            P(("dp", "ctx"), "tensor"),
        ),
        out_specs=(
            P(("dp", "ctx"), None),
            P(("dp", "ctx"), None),
            P(("dp", "ctx"), "tensor"),
            P(("dp", "ctx"), "tensor"),
            P(("dp", "ctx"), "tensor"),
            P(("dp", "ctx"), "tensor"),
            P(("dp", "ctx"), "tensor"),
            P(("dp", "ctx"), "tensor"),
            P(("dp", "ctx"), "tensor"),
            P(("dp", "ctx"), "tensor"),
            P(("dp", "ctx"), "tensor"),
            P(("dp", "ctx"), "tensor"),
            P(("dp", "ctx"), "tensor"),
            P(("dp", "ctx"), "tensor"),
            P(("dp", "ctx"), "tensor"),
            P(("dp", "ctx"), "tensor"),
            P(None, ("dp", "ctx")),
            P(None, ("dp", "ctx")),
        ),
        check_vma=False,
    )
```
